32 devices in a mesh: row: 4 (over y, x), col: 8 (over z, core).
Axes of the slice: x: 2, y: 2, z: 4, core: 2. Of those that a mesh axis runs over, the one named last changes fastest.
Arguments:
- contacts: bfloat16 [256, 256, 256], P('row', 'col'), may hold values from -6 to 6
- w_first: bfloat16 [3, 3, 256, 256], replicated, may hold values from -0.1875 to 0.1875
- w_second: bfloat16 [3, 3, 256, 256], replicated, may hold values from -0.1875 to 0.1875
- w_third: bfloat16 [3, 3, 256, 256], replicated, may hold values from -0.1875 to 0.1875
Outputs:
- features: bfloat16 [256, 256, 256], P('row', 'col')
The draws below stay inside these ranges and needn't reach their ends.
All inputs are finite; a program needn't handle non-finite values.
Results may differ from the reference program's by a relative error of at most 0.0064.
Values may be sent and summed in bfloat16 or wider, within the bound.
No kernel may reach another device: no remote copies, remote signals or barrier semaphores. Data moves between devices by JAX's collectives and lax.ppermute only.
A program may use at most 64 MiB of HBM per device.

```python
import jax
import jax.numpy as jnp
from jax import lax

C = 256
N = 256


def steps_of(stream_key, dims, shards, smallest, largest):
    def one(axis_at, parts):
        draws = jax.random.uniform(jax.random.fold_in(jax.random.fold_in(stream_key, 6), axis_at), (parts,), jnp.float32, smallest / len(shards), largest / len(shards))
        return jnp.repeat(jnp.exp(draws), dims[axis_at] // parts).reshape((-1,) + (1,) * (len(dims) - axis_at - 1))

    gain = one(*shards[0])
    for cut in shards[1:]:
        gain = gain * one(*cut)
    return gain


def normal_values(own_key, extent, deviation, limit, cuts=(), held_as=jnp.bfloat16):
    values = deviation * jax.random.normal(own_key, extent, jnp.float32)
    if cuts:
        values = values * steps_of(own_key, extent, cuts, -0.22, 0.18)
    return jnp.clip(values, -limit, limit).astype(held_as)


def setup_inputs(seed: int = 0) -> dict:
    arg_keys = jax.random.split(jax.random.key(seed), 5)
    contacts = normal_values(arg_keys[0], (N, N, C), 1.0, 6.0, ((0, 4), (1, 8)))
    w_first = normal_values(arg_keys[1], (3, 3, C, C), (9 * C // 2) ** -0.5, 0.1875)
    w_second = normal_values(arg_keys[2], (3, 3, C, C), (9 * C // 2) ** -0.5, 0.1875)
    w_third = normal_values(arg_keys[3], (3, 3, C, C), (9 * C // 2) ** -0.5, 0.1875)
    return {"contacts": contacts, "w_first": w_first, "w_second": w_second, "w_third": w_third}


def conv_layer(activation, weight, dilation):
    result = lax.conv_general_dilated(
        activation.astype(jnp.float32)[None],
        weight.astype(jnp.float32),
        window_strides=(1, 1),
        padding=((dilation, dilation), (dilation, dilation)),
        rhs_dilation=(dilation, dilation),
        dimension_numbers=("NHWC", "HWIO", "NHWC"),
        precision=lax.Precision.HIGHEST,
    )[0]
    return jnp.maximum(result, 0.0).astype(jnp.bfloat16)


def symmetrize(activation):
    mirrored = jnp.swapaxes(activation, 0, 1)
    return ((activation.astype(jnp.float32) + mirrored.astype(jnp.float32)) * 0.5).astype(jnp.bfloat16)


def reference(contacts, w_first, w_second, w_third):
    first = conv_layer(contacts, w_first, 1)
    second = conv_layer(symmetrize(first), w_second, 2)
    return conv_layer(symmetrize(second), w_third, 4)
```

```python
import math

import jax
import jax.numpy as jnp
import numpy as np
from jax import lax
from jax.sharding import PartitionSpec as P

AXES = ("row", "col")


def paired(length):
    near = [(i, i + 1) for i in range(0, length - 1, 2)]
    far = [(i, i + 1) for i in range(1, length - 1, 2)]
    return [pairs + [(j, i) for i, j in pairs] for pairs in (near, far)]


def extended(array, axis, dim, width):
    size, length = lax.axis_size(axis), array.shape[dim]
    odd = lax.axis_index(axis) % 2
    near, far = paired(size)
    low = jnp.where(odd == 1, 0, length - width)
    to_near = lax.dynamic_slice_in_dim(array, low, width, axis=dim)
    to_far = lax.dynamic_slice_in_dim(array, length - width - low, width, axis=dim)
    from_far = lax.ppermute(to_far, axis, far) if far else jnp.zeros_like(to_far)
    from_near = lax.ppermute(to_near, axis, near)
    before = jnp.where(odd == 1, from_near, from_far)
    after = jnp.where(odd == 1, from_far, from_near)
    return jnp.concatenate([before, array, after], axis=dim)


def patches(padded, dilation):
    rows, cols, channels = padded.shape
    rows, cols = rows - 2 * dilation, cols - 2 * dilation
    windows = [
        padded[p * dilation : p * dilation + rows, q * dilation : q * dilation + cols, :]
        for p in range(3)
        for q in range(3)
    ]
    return jnp.concatenate(windows, axis=2).reshape(rows * cols, 9 * channels)


def convolved(stacked, weight):
    product = jnp.dot(
        stacked, weight.reshape(stacked.shape[1], weight.shape[3]), preferred_element_type=jnp.float32
    )
    return jnp.maximum(product, 0.0)


def routes(row_count):
    low = math.isqrt(row_count)
    first, second = {}, {}
    for r in range(row_count):
        for z in range(row_count):
            a, b, c, d = r // low, r % low, z // low, z % low
            if r == z:
                continue
            via = (r, z) if b == d else ((z, z) if a == c else (c * low + b, z))
            if via != (r, z):
                first[(r, z)] = via
            second.setdefault(via, []).append((z, r))
    if any(len(ends) > 1 for ends in second.values()) or len(set(first.values())) < len(first):
        pairs = [(r, z) for r in range(row_count) for z in range(row_count) if r != z]
        return {}, {(r, z): (z, r) for r, z in pairs}
    return first, {via: ends[0] for via, ends in second.items()}


def transposed(activation, parts):
    tile_rows, tile_cols, channels = activation.shape
    row_count, col_count = lax.axis_size("row"), lax.axis_size("col")
    ratio = col_count // row_count
    first, second = routes(row_count)
    row, col = lax.axis_index("row"), lax.axis_index("col")
    own = col % ratio

    def device(chip, core):
        return chip[0] * col_count + chip[1] * ratio + core

    def pairs(legs, shift):
        return [
            (device(s, k), device(e, (k + shift) % ratio)) for s, e in legs.items() for k in range(ratio)
        ]

    relay = np.zeros((row_count, row_count), bool)
    for via in first.values():
        relay[via] = True
    is_relay = jnp.asarray(relay)[row, col // ratio]
    diagonal = row == col // ratio
    stay = {(i, i): (i, i) for i in range(row_count)}
    step = tile_cols // parts
    blocks = []
    for shift in range(ratio):
        half = lax.dynamic_slice_in_dim(activation, (own + shift) % ratio * tile_cols, tile_cols, 0)
        got = []
        for part in range(parts):
            piece = half[part * step : part * step + step]
            sent = piece
            if first:
                hop = lax.ppermute(piece, AXES, pairs(first, 0))
                sent = jnp.where(is_relay, hop, piece)
            got.append(lax.ppermute(sent, AXES, pairs(second, shift)))
        kept = lax.ppermute(half, AXES, pairs(stay, shift)) if shift else half
        block = jnp.where(diagonal, kept, jnp.concatenate(got, axis=0))
        blocks.append(jnp.transpose(block, (1, 0, 2)))
    ordered = blocks[0]
    mirrored = jnp.concatenate(blocks, axis=0)
    stacked = mirrored.reshape(ratio, tile_cols, tile_cols, channels)
    places = [lax.dynamic_index_in_dim(stacked, (own - j) % ratio, 0, False) for j in range(ratio)]
    return jnp.concatenate(places, axis=0)


def inside(rows, cols, margin):
    row, col = lax.axis_index("row"), lax.axis_index("col")
    tile_rows, tile_cols = rows - 2 * margin, cols - 2 * margin
    y = row * tile_rows - margin + lax.broadcasted_iota(jnp.int32, (rows, cols, 1), 0)
    x = col * tile_cols - margin + lax.broadcasted_iota(jnp.int32, (rows, cols, 1), 1)
    total = lax.axis_size("row") * tile_rows
    return (y >= 0) & (y < total) & (x >= 0) & (x < total)


def local(contacts, w_first, w_second, w_third):
    tile_rows, tile_cols, channels = contacts.shape
    padded = extended(extended(contacts, "col", 1, 1), "row", 0, 1)
    first = convolved(patches(padded, 1), w_first).astype(jnp.bfloat16)
    first = first.reshape(tile_rows, tile_cols, channels)
    mirrored = transposed(first, 2)
    sym = ((first.astype(jnp.float32) + mirrored.astype(jnp.float32)) * 0.5).astype(jnp.bfloat16)
    padded = extended(extended(sym, "col", 1, 6), "row", 0, 6)
    stacked = patches(padded, 2)
    second = convolved(stacked, w_second).astype(jnp.bfloat16).astype(jnp.float32)
    flipped = convolved(stacked, jnp.swapaxes(w_second, 0, 1)).astype(jnp.bfloat16).astype(jnp.float32)
    sym = ((second + flipped) * 0.5).astype(jnp.bfloat16)
    rows, cols = tile_rows + 8, tile_cols + 8
    sym = jnp.where(inside(rows, cols, 4), sym.reshape(rows, cols, channels), 0)
    features = convolved(patches(sym, 4), w_third).astype(jnp.bfloat16)
    return features.reshape(tile_rows, tile_cols, channels)


def solution(mesh):
    return jax.shard_map(
        local,
        mesh=mesh,
        in_specs=(P("row", "col", None), P(), P(), P()),
        out_specs=P("row", "col", None),
        check_vma=False,
    )
```

```python
import math

import jax
import jax.numpy as jnp
import numpy as np
from jax import lax
from jax.experimental import pallas as pl
from jax.experimental.pallas import tpu as pltpu
from jax.sharding import PartitionSpec as P

AXES = ("row", "col")
BF16, F32 = jnp.bfloat16, jnp.float32
STRIP = 8
PAD = 16


def routes(row_count):
    low = math.isqrt(row_count)
    first, second = {}, {}
    for r in range(row_count):
        for z in range(row_count):
            a, b, c, d = r // low, r % low, z // low, z % low
            if r == z:
                continue
            via = (r, z) if b == d else ((z, z) if a == c else (c * low + b, z))
            if via != (r, z):
                first[(r, z)] = via
            second.setdefault(via, []).append((z, r))
    if any(len(ends) > 1 for ends in second.values()) or len(set(first.values())) < len(first):
        return {}, {(r, z): (z, r) for r in range(row_count) for z in range(row_count) if r != z}
    return first, {via: ends[0] for via, ends in second.items()}


class Place:
    def __init__(self):
        self.rows, self.cols = lax.axis_size("row"), lax.axis_size("col")
        self.row, self.col = lax.axis_index("row"), lax.axis_index("col")
        self.core = self.col % 2
        self.up = self.row % 2
        self.diagonal = self.row == self.col // 2
        self.first, self.second = routes(self.rows)

    def chips(self, array, legs):
        pairs = [
            (s[0] * self.cols + s[1] * 2 + k, e[0] * self.cols + e[1] * 2 + k)
            for s, e in legs.items()
            for k in range(2)
        ]
        return lax.ppermute(array, AXES, pairs)

    def carried(self, piece):
        sent = piece
        if self.first:
            relay = np.zeros((self.rows, self.rows), bool)
            for via in self.first.values():
                relay[via] = True
            here = jnp.asarray(relay)[self.row, self.col // 2]
            sent = jnp.where(here, self.chips(piece, self.first), piece)
        return self.chips(sent, self.second)


def pairwise(array, axis, start):
    size = lax.axis_size(axis)
    pairs = [(i, i + 1) for i in range(start, size - 1, 2)]
    if not pairs:
        return jnp.zeros_like(array)
    return lax.ppermute(array, axis, pairs + [(j, i) for i, j in pairs])


def widen(wide, padded, start, width, step):
    channels = padded.shape[2]
    for q in range(3):
        at = start + q * step
        wide[:, :, q * channels : (q + 1) * channels] = padded[:, at : at + width, :]


def products(wide, weight, row, rows, step, flip=False):
    width, channels = wide.shape[1], wide.shape[2] // 3
    taps = [
        wide[pl.ds(row + p * step, rows), :, q * channels : (q + 1) * channels].reshape(
            rows * width, channels
        )
        for p in range(3)
        for q in range(3)
    ]
    if flip:
        taps = [taps[q * 3 + p] for p in range(3) for q in range(3)]
    flat = weight[...].reshape(9 * channels, weight.shape[3])
    return jnp.maximum(jnp.dot(jnp.concatenate(taps, axis=1), flat, preferred_element_type=F32), 0.0)


def own_kernel(tile, near, far, band_near, band_far, weight, out, padded, wide, *, rows_a_step):
    core, up = lax.axis_index("col") % 2, lax.axis_index("row") % 2
    tile_rows, tile_cols, channels = tile.shape
    left, right = PAD - STRIP, PAD + tile_cols
    inner = pl.ds(STRIP, tile_rows)
    padded[inner, PAD:right, :] = tile[...]
    padded[inner, left:PAD, :] = jnp.where(core == 0, far[...], near[...])
    padded[inner, right : right + STRIP, :] = jnp.where(core == 0, near[...], far[...])
    padded[0:STRIP, left : right + STRIP, :] = jnp.where(up == 0, band_far[...], band_near[...])
    padded[pl.ds(STRIP + tile_rows, STRIP), left : right + STRIP, :] = jnp.where(
        up == 0, band_near[...], band_far[...]
    )
    width = out.shape[1]
    widen(wide, padded, left - 1, width, 1)

    def body(i, _):
        row = i * rows_a_step
        value = products(wide, weight, row + 1, rows_a_step, 1)
        out[pl.ds(row, rows_a_step)] = value.astype(BF16).reshape(rows_a_step, width, -1)
        return 0

    lax.fori_loop(0, out.shape[0] // rows_a_step, body, 0)


def band_kernel(kept0, got0, kept1, got1, near, far, to_near, to_far):
    row, col = lax.axis_index("row"), lax.axis_index("col")
    core, up = col % 2, row % 2
    diagonal = row == col // 2
    cols = got0.shape[0] // (2 * STRIP)
    mid = to_near.shape[0] - 4 * STRIP
    base = 2 * STRIP * cols

    def ring(ref_kept, ref_got, at, size):
        return jnp.where(diagonal, ref_kept[at : at + size, :], ref_got[at : at + size, :])

    for side in range(2):
        lo = 0 if side == 0 else cols - STRIP

        def emit(at, value, side=side):
            @pl.when(up == 1 - side)
            def _():
                to_near[at] = value

            @pl.when(up == side)
            def _():
                to_far[at] = value

        mine = core == side
        for y in range(STRIP):
            at = y * cols + lo
            half = STRIP * cols
            a = jnp.where(mine, far[half + at : half + at + STRIP, :], far[at : at + STRIP, :])
            b = jnp.where(mine, near[half + at : half + at + STRIP, :], near[at : at + STRIP, :])
            emit(y, jnp.where(core == 0, a, b))
            emit(3 * STRIP + mid + y, jnp.where(core == 0, b, a))
            for part, to in ((0, STRIP), (1, 2 * STRIP + mid)):
                where = part * half + at
                emit(
                    to + y,
                    jnp.where(
                        mine, ring(kept0, got0, where, STRIP), ring(kept1, got1, where, STRIP)
                    ),
                )
        for y in range(mid):
            at = base + y * STRIP
            emit(
                2 * STRIP + y,
                jnp.where(
                    mine,
                    ring(kept1, got1, at, STRIP),
                    ring(kept1, got1, at + mid * STRIP, STRIP),
                ),
            )


def rest_kernel(
    first, kept0, got0, kept1, got1, kept2, got2, near, far, band_near, band_far,
    w_first, w_second, w_third, out,
    padded, wide, flipped, sym, wide2, sym2, wide3,
    *, steps,
):
    row, col = lax.axis_index("row"), lax.axis_index("col")
    core, up = col % 2, row % 2
    diagonal = row == col // 2
    tile_rows, tile_cols, channels = out.shape
    mid = tile_cols - 2 * STRIP
    base = 2 * STRIP * tile_cols
    halves = channels // 128

    def pick(ref_kept, ref_got, at, size):
        return jnp.where(diagonal, ref_kept[at : at + size, :], ref_got[at : at + size, :])

    for k in range(2):

        @pl.when(core == k)
        def _():
            mine, other = PAD + k * tile_cols, PAD + (1 - k) * tile_cols
            for y in range(STRIP):
                for part, to in ((0, STRIP), (1, 2 * STRIP + mid)):
                    at = (part * STRIP + y) * tile_cols
                    padded[to + y, mine : mine + tile_cols, :] = pick(kept0, got0, at, tile_cols)
                    padded[to + y, other : other + tile_cols, :] = pick(kept1, got1, at, tile_cols)
            inner = tile_cols - STRIP
            edge = tile_rows - STRIP
            for y in range(mid):
                to = 2 * STRIP + y
                at = PAD + edge * k
                padded[to, at : at + STRIP, :] = pick(kept1, got1, base + y * STRIP, STRIP)
                at = PAD + edge * (1 - k)
                padded[to, at : at + STRIP, :] = pick(kept1, got1, base + (mid + y) * STRIP, STRIP)
                at = PAD + STRIP + inner * k
                padded[to, at : at + inner, :] = pick(kept2, got2, y * inner, inner)
                at = PAD + STRIP + inner * (1 - k)
                padded[to, at : at + inner, :] = pick(kept2, got2, (mid + y) * inner, inner)
            above, below = (far, near) if k == 0 else (near, far)
            half = STRIP * tile_cols
            for ref, to in ((above, 0), (below, STRIP + tile_cols)):
                for y in range(STRIP):
                    at = y * tile_cols
                    padded[to + y, other : other + tile_cols, :] = ref[at : at + tile_cols, :]
                    at += half
                    padded[to + y, mine : mine + tile_cols, :] = ref[at : at + tile_cols, :]

    padded[:, PAD - STRIP : PAD, :] = jnp.where(up == 0, band_far[...], band_near[...])
    end = PAD + tile_rows
    padded[:, end : end + STRIP, :] = jnp.where(up == 0, band_near[...], band_far[...])

    length = wide.shape[1]
    widen(wide, padded, PAD - STRIP - 1, length, 1)

    def firsts(i, _):
        at = i * steps[0]
        value = products(wide, w_first, at + 1, steps[0], 1).astype(BF16).astype(F32)
        for j in range(halves):
            to = pl.ds(pl.multiple_of((at + 2) * length, 8), steps[0] * length)
            flipped[j, to, :] = value[:, j * 128 : (j + 1) * 128]
        return 0

    lax.fori_loop(0, (tile_cols + 12) // steps[0], firsts, 0)

    width = first.shape[1]
    total_rows, total_cols = tile_rows * lax.axis_size("row"), tile_cols * lax.axis_size("col")
    x = col * tile_cols - STRIP + lax.broadcasted_iota(jnp.int32, (width, 1), 0)
    valid = (x >= 0) & (x < total_cols)

    def averages(i, _):
        y = row * tile_rows - 6 + i
        turned = jnp.concatenate(
            [flipped[j, pl.ds(i + 2, width, stride=length), :] for j in range(halves)], axis=1
        )
        mean = (first[i].astype(F32) + turned) * 0.5
        ok = valid & (y >= 0) & (y < total_rows)
        sym[i, STRIP : STRIP + width, :] = jnp.where(ok, mean, 0.0).astype(BF16)
        return 0

    lax.fori_loop(0, first.shape[0], averages, 0)

    widen(wide2, sym, STRIP - 2, width, 2)

    def seconds(i, _):
        at = i * steps[1]
        a = products(wide2, w_second, at, steps[1], 2).astype(BF16).astype(F32)
        b = products(wide2, w_second, at, steps[1], 2, flip=True).astype(BF16).astype(F32)
        mean = ((a + b) * 0.5).reshape(steps[1], width, channels)
        y = row * tile_rows - 4 + at + lax.broadcasted_iota(jnp.int32, (steps[1], 1, 1), 0)
        ok = valid.reshape(1, width, 1) & (y >= 0) & (y < total_rows)
        sym2[pl.ds(at, steps[1])] = jnp.where(ok, mean, 0.0).astype(BF16)
        return 0

    lax.fori_loop(0, (tile_rows + 8) // steps[1], seconds, 0)
    widen(wide3, sym2, STRIP - 4, tile_cols, 4)

    def thirds(i, _):
        at = i * steps[2]
        value = products(wide3, w_third, at, steps[2], 4)
        out[pl.ds(at, steps[2])] = value.astype(BF16).reshape(steps[2], tile_cols, channels)
        return 0

    lax.fori_loop(0, tile_rows // steps[2], thirds, 0)


def whole(count):
    return [pl.BlockSpec(memory_space=pltpu.VMEM)] * count


def divisor(number, most):
    return max(d for d in range(1, most + 1) if number % d == 0)


def local(contacts, w_first, w_second, w_third):
    tile_rows, tile_cols, channels = contacts.shape
    place = Place()
    core, up = place.core, place.up
    params = pltpu.CompilerParams(vmem_limit_bytes=48 * 2**20)
    span, stretch = tile_cols + 2 * STRIP, tile_rows + 2 * STRIP

    def flat(array):
        return array.reshape(-1, channels)

    def cut(array, at, size, dim):
        return lax.dynamic_slice_in_dim(array, at, size, dim)

    mine = cut(contacts, core * tile_cols, tile_cols, 0)
    other = pairwise(cut(contacts, (1 - core) * tile_cols, tile_cols, 0), "col", 0)
    edge = tile_cols - STRIP
    ends = [(0, STRIP), (edge, tile_cols)]
    kept0 = flat(jnp.concatenate([mine[a:b] for a, b in ends]))
    mid_mine, mid_other = mine[STRIP:edge], other[STRIP:edge]
    kept1 = jnp.concatenate(
        [flat(other[a:b]) for a, b in ends]
        + [flat(cut(mid_mine, core * edge, STRIP, 1)), flat(cut(mid_other, (1 - core) * edge, STRIP, 1))]
    )
    kept2 = jnp.concatenate(
        [flat(cut(mid_mine, (1 - core) * STRIP, edge, 1)), flat(cut(mid_other, core * STRIP, edge, 1))]
    )
    got0, got1 = place.carried(kept0), place.carried(kept1)

    near = pairwise(cut(contacts, (1 - core) * edge, STRIP, 1), "col", 0)
    far = pairwise(cut(contacts, core * edge, STRIP, 1), "col", 1)
    left, right = jnp.where(core == 0, far, near), jnp.where(core == 0, near, far)

    def band(at):
        return jnp.concatenate([cut(part, at, STRIP, 0) for part in (left, contacts, right)], axis=1)

    last = tile_rows - STRIP
    band_near = pairwise(band((1 - up) * last), "row", 0)
    band_far = pairwise(band(up * last), "row", 1)
    first = pl.pallas_call(
        lambda *refs: own_kernel(*refs, rows_a_step=divisor(tile_rows + 12, 19)),
        out_shape=jax.ShapeDtypeStruct((tile_rows + 12, span, channels), BF16),
        in_specs=whole(6),
        out_specs=whole(1)[0],
        scratch_shapes=[
            pltpu.VMEM((stretch, tile_cols + 2 * PAD, channels), BF16),
            pltpu.VMEM((stretch, span, 3 * channels), BF16),
        ],
        compiler_params=params,
        name="own_first",
    )(contacts, near, far, band_near, band_far, w_first)

    got2 = place.carried(kept2)

    def ends_of(at):
        pieces = []
        for kept, got in ((kept0, got0), (kept1, got1)):
            size = STRIP * tile_cols
            pieces.append(
                jnp.where(place.diagonal, cut(kept, at * size, size, 0), cut(got, at * size, size, 0))
            )
        return jnp.concatenate(pieces)

    near = pairwise(ends_of(1 - core), "col", 0)
    far = pairwise(ends_of(core), "col", 1)
    strip = jax.ShapeDtypeStruct((span, STRIP, channels), BF16)
    to_near, to_far = pl.pallas_call(
        band_kernel,
        out_shape=(strip, strip),
        in_specs=whole(6),
        out_specs=tuple(whole(2)),
        compiler_params=params,
        name="bands",
    )(kept0, got0, kept1, got1, near, far)
    band_near, band_far = pairwise(to_near, "row", 0), pairwise(to_far, "row", 1)
    steps = (divisor(tile_cols + 12, 11), divisor(tile_rows + 8, 12), divisor(tile_rows, 16))
    return pl.pallas_call(
        lambda *refs: rest_kernel(*refs, steps=steps),
        out_shape=jax.ShapeDtypeStruct(contacts.shape, BF16),
        in_specs=whole(14),
        out_specs=whole(1)[0],
        scratch_shapes=[
            pltpu.VMEM((span, tile_rows + 2 * PAD, channels), BF16),
            pltpu.VMEM((span, stretch, 3 * channels), BF16),
            pltpu.VMEM((channels // 128, span * stretch, 128), F32),
            pltpu.VMEM((tile_rows + 12, tile_cols + 2 * PAD, channels), BF16),
            pltpu.VMEM((tile_rows + 12, span, 3 * channels), BF16),
            pltpu.VMEM((tile_rows + 8, span, channels), BF16),
            pltpu.VMEM((tile_rows + 8, tile_cols, 3 * channels), BF16),
        ],
        compiler_params=params,
        name="rest",
    )(
        first, kept0, got0, kept1, got1, kept2, got2, near, far, band_near, band_far,
        w_first, w_second, w_third,
    )


def solution(mesh):
    return jax.shard_map(
        local,
        mesh=mesh,
        in_specs=(P("row", "col", None), P(), P(), P()),
        out_specs=P("row", "col", None),
        check_vma=False,
    )
```

```python
import math

import jax
import jax.numpy as jnp
import numpy as np
from jax import lax
from jax.experimental import pallas as pl
from jax.experimental.pallas import tpu as pltpu
from jax.sharding import PartitionSpec as P

AXES = ("row", "col")
BF16, F32 = jnp.bfloat16, jnp.float32
PAD = 16
STRIP = 8
HALO = 6
EDGE = 6


def routes(row_count):
    low = math.isqrt(row_count)
    first, second = {}, {}
    for r in range(row_count):
        for z in range(row_count):
            a, b, c, d = r // low, r % low, z // low, z % low
            if r == z:
                continue
            via = (r, z) if b == d else ((z, z) if a == c else (c * low + b, z))
            first[(r, z)] = via
            second.setdefault(via, []).append((z, r))
    if any(len(ends) > 1 for ends in second.values()) or len(set(first.values())) < len(first):
        return {}, {(r, z): (z, r) for r in range(row_count) for z in range(row_count) if r != z}
    return first, {via: ends[0] for via, ends in second.items()}


class Place:
    def __init__(self):
        self.rows, self.cols = lax.axis_size("row"), lax.axis_size("col")
        self.row, self.col = lax.axis_index("row"), lax.axis_index("col")
        self.core = self.col % 2
        self.up = self.row % 2
        self.diagonal = self.row == self.col // 2
        self.first, self.second = routes(self.rows)

    def chips(self, array, legs, shift=0):
        pairs = [
            (s[0] * self.cols + s[1] * 2 + k, e[0] * self.cols + e[1] * 2 + (k + shift) % 2)
            for s, e in legs.items()
            for k in range(2)
        ]
        return lax.ppermute(array, AXES, pairs)

    def hop(self, piece):
        return self.chips(piece, self.first) if self.first else piece

    def land(self, hopped, shift=0):
        return self.chips(hopped, self.second, shift)


def pairwise(array, axis, start, name):
    size = lax.axis_size(axis)
    pairs = [(i, i + 1) for i in range(start, size - 1, 2)]
    if not pairs:
        return jnp.zeros_like(array)
    with jax.named_scope(name):
        return lax.ppermute(array, axis, pairs + [(j, i) for i, j in pairs])


def widen(wide, padded, start, width, step):
    channels = padded.shape[2]
    for q in range(3):
        at = start + q * step
        wide[:, :, q * channels : (q + 1) * channels] = padded[:, at : at + width, :]


def products(wide, weight, row, rows, step, flip=False):
    width, channels = wide.shape[1], wide.shape[2] // 3
    taps = [
        wide[pl.ds(row + p * step, rows), :, q * channels : (q + 1) * channels].reshape(
            rows * width, channels
        )
        for p in range(3)
        for q in range(3)
    ]
    if flip:
        taps = [taps[q * 3 + p] for p in range(3) for q in range(3)]
    flat = weight[...].reshape(9 * channels, weight.shape[3])
    return jnp.maximum(jnp.dot(jnp.concatenate(taps, axis=1), flat, preferred_element_type=F32), 0.0)


def stage_kernel(source, out, done):
    copy = pltpu.make_async_copy(source, out, done)
    copy.start()
    copy.wait()


def first_kernel(half, tile, above, below, before, after, weight, out, padded, wide, *, step):
    tile_rows, tile_cols, channels = tile.shape
    rows = out.shape[0]
    end = PAD + tile_cols
    top = half[0] * rows
    padded[1 : 1 + tile_rows, PAD:end, :] = tile[...]
    padded[0, PAD:end, :] = above[...]
    padded[1 + tile_rows, PAD:end, :] = below[...]
    padded[:, PAD - 1 : PAD, :] = before[...].reshape(tile_rows + 2, 1, channels)
    padded[:, end : end + 1, :] = after[...].reshape(tile_rows + 2, 1, channels)
    widen(wide, padded.at[pl.ds(top, rows + 2)], PAD - 1, tile_cols, 1)
    for at in range(0, rows, step):
        value = products(wide, weight, at, step, 1)
        out[at : at + step] = value.astype(BF16).reshape(step, tile_cols, channels)


def mean_kernel(mine, other, swapped, got0, got1, got2, out, block):
    row, col = lax.axis_index("row"), lax.axis_index("col")
    core = col % 2
    diagonal = row == col // 2
    size = mine.shape[0]
    lead = got0.shape[0]
    rest = size - lead

    @pl.when(diagonal)
    def _():
        block[0] = mine[...]
        block[1] = swapped[...]

    @pl.when(jnp.logical_not(diagonal))
    def _():
        block[0, :lead] = got0[...]
        block[0, lead:] = got1[:rest]
        block[1, : lead - rest] = got1[rest:]
        block[1, lead - rest :] = got2[...]

    for i, (half, first) in enumerate(((core, mine), (1 - core, other))):
        turned = jnp.swapaxes(block[i], 0, 1).astype(F32)
        out[pl.ds(half * size, size)] = ((first[...].astype(F32) + turned) * 0.5).astype(BF16)


def second_rows(wide, weight, at, rows, valid):
    a = products(wide, weight, at, rows, 2).astype(BF16).astype(F32)
    b = products(wide, weight, at, rows, 2, flip=True).astype(BF16).astype(F32)
    mean = ((a + b) * 0.5).reshape(rows, wide.shape[1], -1)
    return jnp.where(valid, mean, 0.0).astype(BF16)


def columns_inside(width, tile_cols):
    col = lax.axis_index("col")
    x = col * tile_cols - (width - tile_cols) // 2 + lax.broadcasted_iota(jnp.int32, (1, width, 1), 1)
    return (x >= 0) & (x < tile_cols * lax.axis_size("col"))


def middle_kernel(
    sym, before, after, w_second, w_third, features, tops, bottoms, padded, wide2, sym2, wide3, out, done, *, steps
):
    tile_rows, tile_cols, channels = sym.shape
    end = PAD + tile_cols
    padded[:, PAD:end, :] = sym[...]
    padded[:, PAD - STRIP : PAD, :] = before[...]
    padded[:, end : end + STRIP, :] = after[...]
    width = wide2.shape[1]
    side = (width - tile_cols) // 2
    widen(wide2, padded, PAD - side - 2, width, 2)
    valid = columns_inside(width, tile_cols)
    rows2, rows3 = sym2.shape[0], out.shape[0]

    def seconds(i, _):
        at = i * steps[0]
        sym2[pl.ds(at, steps[0])] = second_rows(wide2, w_second, at, steps[0], valid)
        return 0

    lax.fori_loop(0, rows2 // steps[0], seconds, 0)
    tops[...] = sym2[0:STRIP]
    bottoms[...] = sym2[rows2 - STRIP : rows2]
    widen(wide3, sym2, side - 4, tile_cols, 4)

    def thirds(i, _):
        at = i * steps[1]
        value = products(wide3, w_third, at, steps[1], 4)
        out[pl.ds(at, steps[1])] = value.astype(BF16).reshape(steps[1], tile_cols, channels)
        return 0

    lax.fori_loop(0, rows3 // steps[1], thirds, 0)
    copy = pltpu.make_async_copy(out, features.at[pl.ds(EDGE, rows3)], done)
    copy.start()
    copy.wait()


def edges_kernel(
    _, sym, before, after, above, below, tops, bottoms, w_second, w_third, features,
    padded, wide2, sym2, wide3, out, done,
):
    row = lax.axis_index("row")
    tile_rows, tile_cols, channels = sym.shape
    end = PAD + tile_cols
    width = wide2.shape[1]
    side = (width - tile_cols) // 2
    valid = columns_inside(width, tile_cols)
    near = padded.shape[0] - HALO
    for i in range(2):
        rows = pl.ds(HALO, near) if i == 0 else pl.ds(0, near)
        outside = pl.ds(0, HALO) if i == 0 else pl.ds(near, HALO)
        source = pl.ds(0, near) if i == 0 else pl.ds(tile_rows - near, near)
        padded[rows, PAD:end, :] = sym[source]
        padded[rows, PAD - STRIP : PAD, :] = before[source]
        padded[rows, end : end + STRIP, :] = after[source]
        padded[outside, PAD - STRIP : end + STRIP, :] = (above if i == 0 else below)[...]
        widen(wide2, padded, PAD - side - 2, width, 2)
        y = lax.broadcasted_iota(jnp.int32, (HALO, 1, 1), 0)
        if i == 0:
            inside = row * tile_rows - 4 + y >= 0
        else:
            inside = (row + 1) * tile_rows - 2 + y < tile_rows * lax.axis_size("row")
        value = second_rows(wide2, w_second, 0, HALO, valid & inside)
        if i == 0:
            sym2[0:HALO], sym2[HALO:] = value, tops[...]
        else:
            sym2[0:STRIP], sym2[STRIP:] = bottoms[...], value
        widen(wide3, sym2, side - 4, tile_cols, 4)
        value = products(wide3, w_third, 0, EDGE, 4)
        out[i] = value.astype(BF16).reshape(EDGE, tile_cols, channels)
        target = features.at[pl.ds(0 if i == 0 else tile_rows - EDGE, EDGE)]
        pltpu.make_async_copy(out.at[i], target, done.at[i]).start()
    for i in range(2):
        target = features.at[pl.ds(0 if i == 0 else tile_rows - EDGE, EDGE)]
        pltpu.make_async_copy(out.at[i], target, done.at[i]).wait()


def whole(count):
    return [pl.BlockSpec(memory_space=pltpu.VMEM)] * count


def divisor(number, most):
    return max(d for d in range(1, most + 1) if number % d == 0)


def cut(array, at, size, dim):
    return lax.dynamic_slice_in_dim(array, at, size, dim)


def local(contacts, w_first, w_second, w_third):
    tile_rows, tile_cols, channels = contacts.shape
    place = Place()
    core, up = place.core, place.up
    params = pltpu.CompilerParams(vmem_limit_bytes=32 * 2**20)
    anywhere = pl.BlockSpec(memory_space=pl.ANY)

    def shape(*dims):
        return jax.ShapeDtypeStruct((*dims, channels), BF16)

    def scratch(*dims):
        return pltpu.VMEM(dims, BF16)

    def cost(pixels):
        macs = pixels * 9 * channels * channels
        return pl.CostEstimate(flops=2 * macs, bytes_accessed=9 * channels * channels * 2, transcendentals=0)

    tile = pl.pallas_call(
        stage_kernel,
        out_shape=shape(tile_rows, tile_cols),
        in_specs=[anywhere],
        out_specs=whole(1)[0],
        scratch_shapes=[pltpu.SemaphoreType.DMA],
        compiler_params=params,
        name="stage",
    )(contacts)

    ends = [tile[0], tile[tile_rows - 1]]
    band_near = pairwise(jnp.where(up == 0, ends[1], ends[0]), "row", 0, "own_band_near")
    band_far = pairwise(jnp.where(up == 0, ends[0], ends[1]), "row", 1, "own_band_far")
    above, below = jnp.where(up == 0, band_far, band_near), jnp.where(up == 0, band_near, band_far)
    ends = [
        jnp.concatenate([above[x : x + 1], tile[:, x], below[x : x + 1]]) for x in (0, tile_cols - 1)
    ]
    near = pairwise(jnp.where(core == 0, ends[1], ends[0]), "col", 0, "own_near")
    far = pairwise(jnp.where(core == 0, ends[0], ends[1]), "col", 1, "own_far")
    before, after = jnp.where(core == 0, far, near), jnp.where(core == 0, near, far)

    def first_of(half):
        return pl.pallas_call(
            lambda *refs: first_kernel(*refs, step=tile_cols // 2),
            out_shape=shape(tile_cols, tile_cols),
            in_specs=[pl.BlockSpec(memory_space=pltpu.SMEM)] + whole(6),
            out_specs=whole(1)[0],
            scratch_shapes=[
                scratch(tile_rows + 2, tile_cols + 2 * PAD, channels),
                scratch(tile_cols + 2, tile_cols, 3 * channels),
            ],
            compiler_params=params,
            cost_estimate=cost(tile_cols * tile_cols),
            name="first",
        )(half.reshape(1), tile, above, below, before, after, w_first)

    mine, other = first_of(core), first_of(1 - core)
    lead = tile_cols * 11 // 16
    with jax.named_scope("hop0"):
        hop0 = place.hop(mine[:lead])
    swapped = pairwise(other, "col", 0, "swap")
    with jax.named_scope("hop1"):
        hop1 = place.hop(jnp.concatenate([mine[lead:], swapped[: 2 * lead - tile_cols]]))
    with jax.named_scope("hop2"):
        hop2 = place.hop(swapped[2 * lead - tile_cols :])
    with jax.named_scope("land0"):
        got0 = place.land(hop0)
    with jax.named_scope("land1"):
        got1 = place.land(hop1)
    with jax.named_scope("land2"):
        got2 = place.land(hop2)
    sym = pl.pallas_call(
        mean_kernel,
        out_shape=shape(tile_rows, tile_cols),
        in_specs=whole(6),
        out_specs=whole(1)[0],
        scratch_shapes=[scratch(2, tile_cols, tile_cols, channels)],
        compiler_params=params,
        name="mean",
    )(mine, other, swapped, got0, got1, got2)

    last = tile_cols - STRIP
    near = pairwise(cut(sym, (1 - core) * last, STRIP, 1), "col", 0, "sym_near")
    far = pairwise(cut(sym, core * last, STRIP, 1), "col", 1, "sym_far")
    before, after = jnp.where(core == 0, far, near), jnp.where(core == 0, near, far)

    def band(at):
        return jnp.concatenate([cut(part, at, HALO, 0) for part in (before, sym, after)], axis=1)

    last = tile_rows - HALO
    band_near = pairwise(band((1 - up) * last), "row", 0, "sym_band_near")
    band_far = pairwise(band(up * last), "row", 1, "sym_band_far")
    width = tile_cols + 2 * STRIP
    rows2, rows3 = tile_rows - 4, tile_rows - 2 * EDGE
    features, tops, bottoms = pl.pallas_call(
        lambda *refs: middle_kernel(*refs, steps=(divisor(rows2, 20), divisor(rows3, 26))),
        out_shape=(shape(tile_rows, tile_cols), shape(STRIP, width), shape(STRIP, width)),
        in_specs=whole(5),
        out_specs=(anywhere, *whole(2)),
        scratch_shapes=[
            scratch(tile_rows, tile_cols + 2 * PAD, channels),
            scratch(tile_rows, width, 3 * channels),
            scratch(rows2, width, channels),
            scratch(rows2, tile_cols, 3 * channels),
            scratch(rows3, tile_cols, channels),
            pltpu.SemaphoreType.DMA,
        ],
        compiler_params=params,
        cost_estimate=cost(2 * rows2 * width + rows3 * tile_cols),
        name="middle",
    )(sym, before, after, w_second, w_third)
    above, below = jnp.where(up == 0, band_far, band_near), jnp.where(up == 0, band_near, band_far)
    return pl.pallas_call(
        edges_kernel,
        out_shape=shape(tile_rows, tile_cols),
        in_specs=[anywhere] + whole(9),
        out_specs=anywhere,
        scratch_shapes=[
            scratch(HALO + 4, tile_cols + 2 * PAD, channels),
            scratch(HALO + 4, width, 3 * channels),
            scratch(HALO + STRIP, width, channels),
            scratch(HALO + STRIP, tile_cols, 3 * channels),
            scratch(2, EDGE, tile_cols, channels),
            pltpu.SemaphoreType.DMA((2,)),
        ],
        input_output_aliases={0: 0},
        compiler_params=params,
        cost_estimate=cost(2 * 2 * HALO * width + 2 * EDGE * tile_cols),
        name="edges",
    )(features, sym, before, after, above, below, tops, bottoms, w_second, w_third)


def solution(mesh):
    return jax.shard_map(
        local,
        mesh=mesh,
        in_specs=(P("row", "col", None), P(), P(), P()),
        out_specs=P("row", "col", None),
        check_vma=False,
    )
```

```python
import math

import jax
import jax.numpy as jnp
import numpy as np
from jax import lax
from jax.experimental import pallas as pl
from jax.experimental.pallas import tpu as pltpu
from jax.sharding import PartitionSpec as P

AXES = ("row", "col")
BF16, F32 = jnp.bfloat16, jnp.float32
PAD = 16
STRIP = 8
HALO = 6
EDGE = 6


def routes(row_count):
    low = math.isqrt(row_count)
    first, second = {}, {}
    for r in range(row_count):
        for z in range(row_count):
            a, b, c, d = r // low, r % low, z // low, z % low
            if r == z:
                continue
            via = (r, z) if b == d else ((z, z) if a == c else (c * low + b, z))
            first[(r, z)] = via
            second.setdefault(via, []).append((z, r))
    if any(len(ends) > 1 for ends in second.values()) or len(set(first.values())) < len(first):
        return {}, {(r, z): (z, r) for r in range(row_count) for z in range(row_count) if r != z}
    return first, {via: ends[0] for via, ends in second.items()}


class Place:
    def __init__(self):
        self.rows, self.cols = lax.axis_size("row"), lax.axis_size("col")
        self.row, self.col = lax.axis_index("row"), lax.axis_index("col")
        self.core = self.col % 2
        self.up = self.row % 2
        self.diagonal = self.row == self.col // 2
        self.first, self.second = routes(self.rows)

    def chips(self, array, legs, shift=0):
        pairs = [
            (s[0] * self.cols + s[1] * 2 + k, e[0] * self.cols + e[1] * 2 + (k + shift) % 2)
            for s, e in legs.items()
            for k in range(2)
        ]
        return lax.ppermute(array, AXES, pairs)

    def hop(self, piece):
        return self.chips(piece, self.first) if self.first else piece

    def land(self, hopped, shift=0):
        return self.chips(hopped, self.second, shift)


def pairwise(array, axis, start, name):
    size = lax.axis_size(axis)
    pairs = [(i, i + 1) for i in range(start, size - 1, 2)]
    if not pairs:
        return jnp.zeros_like(array)
    with jax.named_scope(name):
        return lax.ppermute(array, axis, pairs + [(j, i) for i, j in pairs])


def widen(wide, padded, start, width, step):
    channels = padded.shape[2]
    for q in range(3):
        at = start + q * step
        wide[:, :, q * channels : (q + 1) * channels] = padded[:, at : at + width, :]


def products(wide, weight, row, rows, step, flip=False):
    width, channels = wide.shape[1], wide.shape[2] // 3
    taps = [
        wide[pl.ds(row + p * step, rows), :, q * channels : (q + 1) * channels].reshape(
            rows * width, channels
        )
        for p in range(3)
        for q in range(3)
    ]
    if flip:
        taps = [taps[q * 3 + p] for p in range(3) for q in range(3)]
    flat = weight[...].reshape(9 * channels, weight.shape[3])
    return jnp.maximum(jnp.dot(jnp.concatenate(taps, axis=1), flat, preferred_element_type=F32), 0.0)


def stage_kernel(source, out, done):
    copy = pltpu.make_async_copy(source, out, done)
    copy.start()
    copy.wait()


def sides(near, far):
    core = lax.axis_index("col") % 2
    return jnp.where(core == 0, far, near), jnp.where(core == 0, near, far)


def put_tile(padded, tile, near, far):
    rows, cols, channels = tile.shape
    padded[1 : 1 + rows, PAD : PAD + cols, :] = tile[...]
    before, after = sides(near[...], far[...])
    padded[1 : 1 + rows, PAD - 1 : PAD, :] = before.reshape(rows, 1, channels)
    padded[1 : 1 + rows, PAD + cols : PAD + cols + 1, :] = after.reshape(rows, 1, channels)


def inner_first_kernel(tile, near, far, weight, out, padded, wide):
    rows, cols, channels = out.shape
    put_tile(padded, tile, near, far)
    at = lax.axis_index("col") % 2 * cols + (cols - rows) // 2
    widen(wide, padded.at[pl.ds(at, rows + 2)], PAD - 1, cols, 1)
    out[...] = products(wide, weight, 0, rows, 1).astype(BF16).reshape(rows, cols, channels)


def outer_first_kernel(tile, near, far, band_near, band_far, weight, mine, other, padded, wide):
    core, up = lax.axis_index("col") % 2, lax.axis_index("row") % 2
    rows, cols, channels = tile.shape
    put_tile(padded, tile, near, far)
    ends = slice(PAD - 1, PAD + cols + 1)
    padded[0, ends, :] = jnp.where(up == 0, band_far[...], band_near[...])
    padded[rows + 1, ends, :] = jnp.where(up == 0, band_near[...], band_far[...])
    inset = mine.shape[0] // 2
    top = core * cols
    pieces = [
        (top, inset, mine.at[:inset]),
        (top + cols - inset, inset, mine.at[inset:]),
        ((1 - core) * cols, cols, other),
    ]
    to = 0
    for at, count, _ in pieces:
        widen(wide.at[to : to + count + 2], padded.at[pl.ds(at, count + 2)], PAD - 1, cols, 1)
        to += count + 2
    to = 0
    for _, count, out in pieces:
        value = products(wide, weight, to, count, 1)
        out[...] = value.astype(BF16).reshape(count, cols, channels)
        to += count + 2


def mean_kernel(inner, outer, other, swapped, got0, got1, got2, out, to_near, to_far, block):
    row, col = lax.axis_index("row"), lax.axis_index("col")
    core = col % 2
    diagonal = row == col // 2
    size = other.shape[0]
    inset = outer.shape[0] // 2
    over = size - got2.shape[0]

    def put(to, inner, outer):
        to[inset : size - inset] = inner[...]
        to[:inset] = outer[:inset]
        to[size - inset :] = outer[inset : 2 * inset]

    @pl.when(diagonal)
    def _():
        put(block.at[0], inner, outer)
        block[1] = swapped[...]

    @pl.when(jnp.logical_not(diagonal))
    def _():
        put(block.at[0], got0, got1)
        block[1, :over] = got1[2 * inset :]
        block[1, over:] = got2[...]

    def mean(first, turned):
        return ((first.astype(F32) + turned.astype(F32)) * 0.5).astype(BF16)

    turned = jnp.swapaxes(block[0], 0, 1)
    half = core * size
    out[pl.ds(half + inset, size - 2 * inset)] = mean(inner[...], turned[inset : size - inset])
    out[pl.ds(half, inset)] = mean(outer[:inset], turned[:inset])
    out[pl.ds(half + size - inset, inset)] = mean(outer[inset:], turned[size - inset :])
    out[pl.ds((1 - core) * size, size)] = mean(other[...], jnp.swapaxes(block[1], 0, 1))
    start, end = out[:, :STRIP, :], out[:, size - STRIP :, :]
    to_near[...] = jnp.where(core == 0, end, start)
    to_far[...] = jnp.where(core == 0, start, end)


def second_rows(wide, weight, at, rows, valid):
    a = products(wide, weight, at, rows, 2).astype(BF16).astype(F32)
    b = products(wide, weight, at, rows, 2, flip=True).astype(BF16).astype(F32)
    mean = ((a + b) * 0.5).reshape(rows, wide.shape[1], -1)
    return jnp.where(valid, mean, 0.0).astype(BF16)


def columns_inside(x, tile_cols):
    x = x + lax.axis_index("col") * tile_cols
    return (x >= 0) & (x < tile_cols * lax.axis_size("col"))


def inner_second_kernel(sym, weight, out, wide, *, step):
    cols, channels = sym.shape[1], sym.shape[2]
    wide[:, 2:, :channels] = sym[:, : cols - 2, :]
    wide[:, :, channels : 2 * channels] = sym[...]
    wide[:, : cols - 2, 2 * channels :] = sym[:, 2:, :]
    for at in range(0, out.shape[0], step):
        out[at : at + step] = second_rows(wide, weight, at, step, True)


def middle_kernel(
    sym, near, far, inner, w_second, w_third, features, tops, bottoms, padded, wide2, sym2, wide3, out, done,
    *, steps
):
    tile_rows, tile_cols, channels = sym.shape
    end = PAD + tile_cols
    padded[:, PAD:end, :] = sym[...]
    before, after = sides(near[...], far[...])
    padded[:, PAD - STRIP : PAD, :] = before
    padded[:, end : end + STRIP, :] = after
    half = wide2.shape[1] // 2
    for q in range(3):
        lanes = slice(q * channels, (q + 1) * channels)
        at = PAD - 6 + 2 * q
        wide2[:, :half, lanes] = padded[:, at : at + half, :]
        at += tile_cols
        wide2[:, half:, lanes] = padded[:, at : at + half, :]
    x = lax.broadcasted_iota(jnp.int32, (1, 2 * half, 1), 1)
    valid = columns_inside(jnp.where(x < half, x - 4, x - half + tile_cols - 4), tile_cols)
    rows2, rows3 = sym2.shape[0], out.shape[0]
    sym2[:, STRIP : STRIP + tile_cols, :] = inner[...]
    for at in range(0, rows2, steps[0]):
        value = second_rows(wide2, w_second, at, steps[0], valid)
        rows = slice(at, at + steps[0])
        sym2[rows, STRIP - 4 : STRIP - 4 + half, :] = value[:, :half, :]
        to = STRIP + tile_cols - 4
        sym2[rows, to : to + half, :] = value[:, half:, :]
    tops[...] = sym2[0:STRIP]
    bottoms[...] = sym2[rows2 - STRIP : rows2]
    widen(wide3, sym2, STRIP - 4, tile_cols, 4)
    copies = []
    for i, at in enumerate(range(0, rows3, steps[1])):
        value = products(wide3, w_third, at, steps[1], 4)
        rows = pl.ds(at, steps[1])
        out[rows] = value.astype(BF16).reshape(steps[1], tile_cols, channels)
        target = features.at[pl.ds(EDGE + at, steps[1])]
        copies.append(pltpu.make_async_copy(out.at[rows], target, done.at[i]))
        copies[-1].start()
    for copy in copies:
        copy.wait()


def edges_kernel(
    _, sym, near, far, band_near, band_far, tops, bottoms, w_second, w_third, features,
    padded, wide2, sym2, wide3, out, done,
):
    row = lax.axis_index("row")
    up = row % 2
    tile_rows, tile_cols, channels = sym.shape
    end = PAD + tile_cols
    width = wide2.shape[2]
    side = (width - tile_cols) // 2
    x = lax.broadcasted_iota(jnp.int32, (1, width, 1), 1) - side
    valid = columns_inside(x, tile_cols)
    rows = padded.shape[1] - HALO
    bands = (
        jnp.where(up == 0, band_far[...], band_near[...]),
        jnp.where(up == 0, band_near[...], band_far[...]),
    )
    targets = [features.at[pl.ds(0, EDGE)], features.at[pl.ds(tile_rows - EDGE, EDGE)]]
    copies = [pltpu.make_async_copy(out.at[i], targets[i], done.at[i]) for i in range(2)]
    y = lax.broadcasted_iota(jnp.int32, (HALO, 1, 1), 0)
    insides = [
        row * tile_rows - 4 + y >= 0,
        (row + 1) * tile_rows - 2 + y < tile_rows * lax.axis_size("row"),
    ]
    for i in range(2):
        own = slice(HALO, HALO + rows) if i == 0 else slice(0, rows)
        outside = slice(0, HALO) if i == 0 else slice(rows, rows + HALO)
        source = slice(0, rows) if i == 0 else slice(tile_rows - rows, tile_rows)
        padded[i, own, PAD:end, :] = sym[source]
        before, after = sides(near[source], far[source])
        padded[i, own, PAD - STRIP : PAD, :] = before
        padded[i, own, end : end + STRIP, :] = after
        padded[i, outside, PAD - STRIP : end + STRIP, :] = bands[i]
        widen(wide2.at[i], padded.at[i], PAD - side - 2, width, 2)
    values = [second_rows(wide2.at[i], w_second, 0, HALO, valid & insides[i]) for i in range(2)]
    sym2[0, 0:HALO], sym2[0, HALO:] = values[0], tops[...]
    sym2[1, 0:STRIP], sym2[1, STRIP:] = bottoms[...], values[1]
    for i in range(2):
        widen(wide3.at[i], sym2.at[i], side - 4, tile_cols, 4)
    for i in range(2):
        value = products(wide3.at[i], w_third, 0, EDGE, 4)
        out[i] = value.astype(BF16).reshape(EDGE, tile_cols, channels)
        copies[i].start()
    for copy in copies:
        copy.wait()


def whole(count):
    return [pl.BlockSpec(memory_space=pltpu.VMEM)] * count


def divisor(number, most):
    return max(d for d in range(1, most + 1) if number % d == 0)


def cut(array, at, size, dim):
    return lax.dynamic_slice_in_dim(array, at, size, dim)


def local(contacts, w_first, w_second, w_third):
    tile_rows, tile_cols, channels = contacts.shape
    place = Place()
    core, up = place.core, place.up
    anywhere = pl.BlockSpec(memory_space=pl.ANY)

    def shape(*dims):
        return jax.ShapeDtypeStruct((*dims, channels), BF16)

    def scratch(*dims):
        return pltpu.VMEM(dims, BF16)

    def call(name, kernel, outs, ins, scratches, pixels=0, in_specs=None, out_specs=None, alias=None):
        macs = pixels * 9 * channels * channels
        return pl.pallas_call(
            kernel,
            out_shape=outs,
            in_specs=in_specs or whole(len(ins)),
            out_specs=out_specs or tuple(whole(len(outs))),
            scratch_shapes=scratches,
            input_output_aliases=alias or {},
            compiler_params=pltpu.CompilerParams(vmem_limit_bytes=24 * 2**20),
            cost_estimate=pl.CostEstimate(
                flops=2 * macs, bytes_accessed=18 * channels * channels, transcendentals=0
            ),
            name=name,
        )(*ins)

    (tile,) = call(
        "stage",
        stage_kernel,
        (shape(tile_rows, tile_cols),),
        (contacts,),
        [pltpu.SemaphoreType.DMA],
        in_specs=[anywhere],
    )

    ends = [contacts[:, 0], contacts[:, tile_cols - 1]]
    near = pairwise(jnp.where(core == 0, ends[1], ends[0]), "col", 0, "own_near")
    far = pairwise(jnp.where(core == 0, ends[0], ends[1]), "col", 1, "own_far")
    inset = tile_cols // 8
    lead = tile_cols - 2 * inset
    padded = scratch(tile_rows + 2, tile_cols + 2 * PAD, channels)
    (inner,) = call(
        "inner_first",
        inner_first_kernel,
        (shape(lead, tile_cols),),
        (tile, near, far, w_first),
        [padded, scratch(lead + 2, tile_cols, 3 * channels)],
        lead * tile_cols,
    )
    with jax.named_scope("hop0"):
        hop0 = place.hop(inner)
    before, after = sides(near, far)
    before, after, inner = lax.optimization_barrier((before, after, inner))
    ends = [
        jnp.concatenate([before[y : y + 1], tile[y], after[y : y + 1]]) for y in (0, tile_rows - 1)
    ]
    band_near = pairwise(jnp.where(up == 0, ends[1], ends[0]), "row", 0, "own_band_near")
    band_far = pairwise(jnp.where(up == 0, ends[0], ends[1]), "row", 1, "own_band_far")
    outer, other = call(
        "outer_first",
        outer_first_kernel,
        (shape(2 * inset, tile_cols), shape(tile_cols, tile_cols)),
        (tile, near, far, band_near, band_far, w_first),
        [padded, scratch(2 * inset + tile_cols + 6, tile_cols, 3 * channels)],
        0,
    )
    swapped = pairwise(other, "col", 0, "swap")
    over = tile_cols // 2 - inset
    with jax.named_scope("hop1"):
        hop1 = place.hop(jnp.concatenate([outer, swapped[:over]]))
    with jax.named_scope("hop2"):
        hop2 = place.hop(swapped[over:])
    with jax.named_scope("land0"):
        got0 = place.land(hop0)
    with jax.named_scope("land1"):
        got1 = place.land(hop1)
    with jax.named_scope("land2"):
        got2 = place.land(hop2)
    sym, to_near, to_far = call(
        "mean",
        mean_kernel,
        (shape(tile_rows, tile_cols), shape(tile_rows, STRIP), shape(tile_rows, STRIP)),
        (inner, outer, other, swapped, got0, got1, got2),
        [scratch(2, tile_cols, tile_cols, channels)],
    )

    near = pairwise(to_near, "col", 0, "sym_near")
    far = pairwise(to_far, "col", 1, "sym_far")
    rows2, rows3 = tile_rows - 4, tile_rows - 2 * EDGE
    (inner,) = call(
        "inner_second",
        lambda *refs: inner_second_kernel(*refs, step=divisor(rows2, 20)),
        (shape(rows2, tile_cols),),
        (sym, w_second),
        [scratch(tile_rows, tile_cols, 3 * channels)],
        2 * rows2 * tile_cols,
    )
    before, after = sides(near, far)

    def band(at):
        return jnp.concatenate([cut(part, at, HALO, 0) for part in (before, sym, after)], axis=1)

    last = tile_rows - HALO
    band_near = pairwise(band((1 - up) * last), "row", 0, "sym_band_near")
    band_far = pairwise(band(up * last), "row", 1, "sym_band_far")
    width = tile_cols + 2 * STRIP
    step = divisor(rows3, 26)
    features, tops, bottoms = call(
        "middle",
        lambda *refs: middle_kernel(*refs, steps=(divisor(rows2, 30), step)),
        (shape(tile_rows, tile_cols), shape(STRIP, width), shape(STRIP, width)),
        (sym, near, far, inner, w_second, w_third),
        [
            scratch(tile_rows, tile_cols + 2 * PAD, channels),
            scratch(tile_rows, 16, 3 * channels),
            scratch(rows2, width, channels),
            scratch(rows2, tile_cols, 3 * channels),
            scratch(rows3, tile_cols, channels),
            pltpu.SemaphoreType.DMA((rows3 // step,)),
        ],
        2 * rows2 * 16 + rows3 * tile_cols,
        out_specs=(anywhere, *whole(2)),
    )
    return call(
        "edges",
        edges_kernel,
        (shape(tile_rows, tile_cols),),
        (features, sym, near, far, band_near, band_far, tops, bottoms, w_second, w_third),
        [
            scratch(2, HALO + 4, tile_cols + 2 * PAD, channels),
            scratch(2, HALO + 4, width, 3 * channels),
            scratch(2, HALO + STRIP, width, channels),
            scratch(2, HALO + STRIP, tile_cols, 3 * channels),
            scratch(2, EDGE, tile_cols, channels),
            pltpu.SemaphoreType.DMA((2,)),
        ],
        2 * 2 * HALO * width + 2 * EDGE * tile_cols,
        in_specs=[anywhere] + whole(9),
        out_specs=(anywhere,),
        alias={0: 0},
    )[0]


def solution(mesh):
    return jax.shard_map(
        local,
        mesh=mesh,
        in_specs=(P("row", "col", None), P(), P(), P()),
        out_specs=P("row", "col", None),
        check_vma=False,
    )
```

```python
import math

import jax
import jax.numpy as jnp
import numpy as np
from jax import lax
from jax.experimental import pallas as pl
from jax.experimental.pallas import tpu as pltpu
from jax.sharding import PartitionSpec as P

AXES = ("row", "col")
BF16, F32 = jnp.bfloat16, jnp.float32
PAD = 16
STRIP = 8
HALO = 6
EDGE = 6


def routes(row_count, plan):
    low = math.isqrt(row_count)
    first, second = {}, {}
    for r in range(row_count):
        for z in range(row_count):
            a, b, c, d = r // low, r % low, z // low, z % low
            if r == z:
                continue
            straight, across = (b == d, a == c) if plan == 0 else (a == c, b == d)
            turn = c * low + b if plan == 0 else a * low + d
            via = (r if straight else z if across else turn, z)
            first[(r, z)] = via
            second.setdefault(via, []).append((z, r))
    if any(len(ends) > 1 for ends in second.values()) or len(set(first.values())) < len(first):
        return {}, {(r, z): (z, r) for r in range(row_count) for z in range(row_count) if r != z}
    return first, {via: ends[0] for via, ends in second.items()}


class Place:
    def __init__(self):
        self.rows, self.cols = lax.axis_size("row"), lax.axis_size("col")
        self.row, self.col = lax.axis_index("row"), lax.axis_index("col")
        self.core = self.col % 2
        self.up = self.row % 2
        self.diagonal = self.row == self.col // 2
        self.legs = [routes(self.rows, plan) for plan in range(2)]

    def chips(self, array, legs):
        pairs = [
            (s[0] * self.cols + s[1] * 2 + k, e[0] * self.cols + e[1] * 2 + k)
            for s, e in legs.items()
            for k in range(2)
        ]
        return lax.ppermute(array, AXES, pairs)

    def hop(self, piece, plan):
        first = self.legs[plan][0]
        return self.chips(piece, first) if first else piece

    def direct(self, piece):
        places = [(r, z) for r in range(self.rows) for z in range(self.rows) if r != z]
        return self.chips(piece, {(r, z): (z, r) for r, z in places})

    def land(self, hopped, plan):
        return self.chips(hopped, self.legs[plan][1])


def pairwise(array, axis, start, name):
    size = lax.axis_size(axis)
    pairs = [(i, i + 1) for i in range(start, size - 1, 2)]
    if not pairs:
        return jnp.zeros_like(array)
    with jax.named_scope(name):
        return lax.ppermute(array, axis, pairs + [(j, i) for i, j in pairs])


def widen(wide, padded, start, width, step):
    channels = padded.shape[2]
    for q in range(3):
        at = start + q * step
        wide[:, :, q * channels : (q + 1) * channels] = padded[:, at : at + width, :]


def products(wide, weight, row, rows, step, flip=False):
    width, channels = wide.shape[1], wide.shape[2] // 3
    taps = [
        wide[pl.ds(row + p * step, rows), :, q * channels : (q + 1) * channels].reshape(
            rows * width, channels
        )
        for p in range(3)
        for q in range(3)
    ]
    if flip:
        taps = [taps[q * 3 + p] for p in range(3) for q in range(3)]
    flat = weight[...].reshape(9 * channels, weight.shape[3])
    return jnp.maximum(jnp.dot(jnp.concatenate(taps, axis=1), flat, preferred_element_type=F32), 0.0)


def sides(near, far):
    core = lax.axis_index("col") % 2
    return jnp.where(core == 0, far, near), jnp.where(core == 0, near, far)


def put_tile(padded, tile, near, far):
    rows, cols, channels = tile.shape
    padded[1 : 1 + rows, PAD : PAD + cols, :] = tile[...]
    before, after = sides(near[...], far[...])
    padded[1 : 1 + rows, PAD - 1 : PAD, :] = before.reshape(rows, 1, channels)
    padded[1 : 1 + rows, PAD + cols : PAD + cols + 1, :] = after.reshape(rows, 1, channels)


def first_kernel(tile, near, far, band_near, band_far, weight, out, mine, other, padded, wide, *, step):
    core, up = lax.axis_index("col") % 2, lax.axis_index("row") % 2
    rows, cols, channels = tile.shape
    put_tile(padded, tile, near, far)
    ends = slice(PAD - 1, PAD + cols + 1)
    padded[0, ends, :] = jnp.where(up == 0, band_far[...], band_near[...])
    padded[rows + 1, ends, :] = jnp.where(up == 0, band_near[...], band_far[...])
    widen(wide, padded, PAD - 1, cols, 1)
    for at in range(0, rows, step):
        value = products(wide, weight, at, step, 1)
        out[at : at + step] = value.astype(BF16).reshape(step, cols, channels)
    outer = jnp.where(core == 0, out[:, 0, :], out[:, cols - 1, :])
    for half in range(2):
        top = half * cols

        def put(ring, top=top):
            ring[:cols] = out[top]
            ring[cols : 2 * cols] = out[top + cols - 1]
            ring[2 * cols :] = outer[top : top + cols]

        pl.when(core == half)(lambda put=put: put(mine))
        pl.when(core != half)(lambda put=put: put(other))


def turned_kernel(kept0, kept1, kept2, kept3, got0, got1, got2, got3, weight, out, padded, wide, *, step):
    core = lax.axis_index("col") % 2
    diagonal = lax.axis_index("row") == lax.axis_index("col") // 2
    size, length, channels = out.shape
    rows = kept0.shape[0]

    def put(pieces):
        for side in range(2):
            left = PAD + side * size

            def fill(first, second, left=left):
                padded[1 : 1 + rows, left : left + size, :] = first[...]
                padded[1 + rows : 1 + size, left : left + size, :] = second[...]

            pl.when(core == side)(lambda fill=fill: fill(pieces[0], pieces[2]))
            pl.when(core != side)(lambda fill=fill: fill(pieces[1], pieces[3]))

    pl.when(diagonal)(lambda: put((kept0, kept1, kept2, kept3)))
    pl.when(jnp.logical_not(diagonal))(lambda: put((got0, got1, got2, got3)))
    widen(wide, padded, PAD - 1, length, 1)
    for at in range(0, size, step):
        value = products(wide, weight, at, step, 1)
        out[at : at + step] = value.astype(BF16).reshape(step, length, channels)


def mean_kernel(first, turned, kept, got, out, to_near, to_far, block, ring):
    row, col = lax.axis_index("row"), lax.axis_index("col")
    core = col % 2
    diagonal = row == col // 2
    size, length, channels = turned.shape
    count = 3 * size
    ring[...] = jnp.where(diagonal, kept[...], got[...])
    block[...] = turned[...]
    for side in range(2):
        left = side * size
        edge = 0 if side == 0 else length - 1

        def put(at, left=left, edge=edge):
            block[0, left : left + size, :] = ring[at : at + size]
            block[size - 1, left : left + size, :] = ring[at + size : at + 2 * size]
            outer = ring[at + 2 * size : at + count]
            block[:, edge : edge + 1, :] = outer.reshape(size, 1, channels)

        pl.when(core == side)(lambda put=put: put(0))
        pl.when(core != side)(lambda put=put: put(count))
    for side in range(2):
        rows = slice(side * size, (side + 1) * size)
        other = jnp.swapaxes(block[:, rows, :], 0, 1).astype(F32)
        out[rows] = ((first[rows].astype(F32) + other) * 0.5).astype(BF16)
    start, end = out[:, :STRIP, :], out[:, size - STRIP :, :]
    to_near[...] = jnp.where(core == 0, end, start)
    to_far[...] = jnp.where(core == 0, start, end)


def second_rows(wide, weight, at, rows, valid):
    a = products(wide, weight, at, rows, 2).astype(BF16).astype(F32)
    b = products(wide, weight, at, rows, 2, flip=True).astype(BF16).astype(F32)
    mean = ((a + b) * 0.5).reshape(rows, wide.shape[1], -1)
    return jnp.where(valid, mean, 0.0).astype(BF16)


def columns_inside(x, tile_cols):
    x = x + lax.axis_index("col") * tile_cols
    return (x >= 0) & (x < tile_cols * lax.axis_size("col"))


def inner_second_kernel(sym, weight, out, wide, *, step):
    cols, channels = sym.shape[1], sym.shape[2]
    wide[:, 2:, :channels] = sym[:, : cols - 2, :]
    wide[:, :, channels : 2 * channels] = sym[...]
    wide[:, : cols - 2, 2 * channels :] = sym[:, 2:, :]
    for at in range(0, out.shape[0], step):
        out[at : at + step] = second_rows(wide, weight, at, step, True)


def middle_kernel(
    sym, near, far, inner, w_second, w_third, features, tops, bottoms, padded, wide2, sym2, wide3, out, done,
    *, steps
):
    tile_rows, tile_cols, channels = sym.shape
    end = PAD + tile_cols
    padded[:, PAD:end, :] = sym[...]
    before, after = sides(near[...], far[...])
    padded[:, PAD - STRIP : PAD, :] = before
    padded[:, end : end + STRIP, :] = after
    half = wide2.shape[1] // 2
    for q in range(3):
        lanes = slice(q * channels, (q + 1) * channels)
        at = PAD - 6 + 2 * q
        wide2[:, :half, lanes] = padded[:, at : at + half, :]
        at += tile_cols
        wide2[:, half:, lanes] = padded[:, at : at + half, :]
    x = lax.broadcasted_iota(jnp.int32, (1, 2 * half, 1), 1)
    valid = columns_inside(jnp.where(x < half, x - 4, x - half + tile_cols - 4), tile_cols)
    rows2, rows3 = sym2.shape[0], out.shape[0]
    sym2[:, STRIP : STRIP + tile_cols, :] = inner[...]
    for at in range(0, rows2, steps[0]):
        value = second_rows(wide2, w_second, at, steps[0], valid)
        rows = slice(at, at + steps[0])
        sym2[rows, STRIP - 4 : STRIP - 4 + half, :] = value[:, :half, :]
        to = STRIP + tile_cols - 4
        sym2[rows, to : to + half, :] = value[:, half:, :]
    tops[...] = sym2[0:STRIP]
    bottoms[...] = sym2[rows2 - STRIP : rows2]
    widen(wide3, sym2, STRIP - 4, tile_cols, 4)
    copies = []
    for i, at in enumerate(range(0, rows3, steps[1])):
        value = products(wide3, w_third, at, steps[1], 4)
        rows = pl.ds(at, steps[1])
        out[rows] = value.astype(BF16).reshape(steps[1], tile_cols, channels)
        target = features.at[pl.ds(EDGE + at, steps[1])]
        copies.append(pltpu.make_async_copy(out.at[rows], target, done.at[i]))
        copies[-1].start()
    for copy in copies:
        copy.wait()


def edges_kernel(
    _, sym, near, far, band_near, band_far, tops, bottoms, w_second, w_third, features,
    padded, wide2, sym2, wide3, out, done,
):
    row = lax.axis_index("row")
    up = row % 2
    tile_rows, tile_cols, channels = sym.shape
    end = PAD + tile_cols
    width = wide2.shape[2]
    side = (width - tile_cols) // 2
    x = lax.broadcasted_iota(jnp.int32, (1, width, 1), 1) - side
    valid = columns_inside(x, tile_cols)
    rows = padded.shape[1] - HALO
    bands = (
        jnp.where(up == 0, band_far[...], band_near[...]),
        jnp.where(up == 0, band_near[...], band_far[...]),
    )
    targets = [features.at[pl.ds(0, EDGE)], features.at[pl.ds(tile_rows - EDGE, EDGE)]]
    copies = [pltpu.make_async_copy(out.at[i], targets[i], done.at[i]) for i in range(2)]
    y = lax.broadcasted_iota(jnp.int32, (HALO, 1, 1), 0)
    insides = [
        row * tile_rows - 4 + y >= 0,
        (row + 1) * tile_rows - 2 + y < tile_rows * lax.axis_size("row"),
    ]
    for i in range(2):
        own = slice(HALO, HALO + rows) if i == 0 else slice(0, rows)
        outside = slice(0, HALO) if i == 0 else slice(rows, rows + HALO)
        source = slice(0, rows) if i == 0 else slice(tile_rows - rows, tile_rows)
        padded[i, own, PAD:end, :] = sym[source]
        before, after = sides(near[source], far[source])
        padded[i, own, PAD - STRIP : PAD, :] = before
        padded[i, own, end : end + STRIP, :] = after
        padded[i, outside, PAD - STRIP : end + STRIP, :] = bands[i]
        widen(wide2.at[i], padded.at[i], PAD - side - 2, width, 2)
    values = [second_rows(wide2.at[i], w_second, 0, HALO, valid & insides[i]) for i in range(2)]
    sym2[0, 0:HALO], sym2[0, HALO:] = values[0], tops[...]
    sym2[1, 0:STRIP], sym2[1, STRIP:] = bottoms[...], values[1]
    for i in range(2):
        widen(wide3.at[i], sym2.at[i], side - 4, tile_cols, 4)
    for i in range(2):
        value = products(wide3.at[i], w_third, 0, EDGE, 4)
        out[i] = value.astype(BF16).reshape(EDGE, tile_cols, channels)
        copies[i].start()
    for copy in copies:
        copy.wait()


def whole(count):
    return [pl.BlockSpec(memory_space=pltpu.VMEM)] * count


def divisor(number, most):
    return max(d for d in range(1, most + 1) if number % d == 0)


def cut(array, at, size, dim):
    return lax.dynamic_slice_in_dim(array, at, size, dim)


def local(contacts, w_first, w_second, w_third):
    tile_rows, tile_cols, channels = contacts.shape
    place = Place()
    core, up = place.core, place.up
    anywhere = pl.BlockSpec(memory_space=pl.ANY)

    def shape(*dims):
        return jax.ShapeDtypeStruct((*dims, channels), BF16)

    def scratch(*dims):
        return pltpu.VMEM(dims, BF16)

    def call(name, kernel, outs, ins, scratches, pixels=0, in_specs=None, out_specs=None, alias=None):
        macs = pixels * 9 * channels * channels
        return pl.pallas_call(
            kernel,
            out_shape=outs,
            in_specs=in_specs or whole(len(ins)),
            out_specs=out_specs or tuple(whole(len(outs))),
            scratch_shapes=scratches,
            input_output_aliases=alias or {},
            compiler_params=pltpu.CompilerParams(vmem_limit_bytes=24 * 2**20),
            cost_estimate=pl.CostEstimate(
                flops=2 * macs, bytes_accessed=18 * channels * channels, transcendentals=0
            ),
            name=name,
        )(*ins)

    tile = contacts
    mine = cut(tile, core * tile_cols, tile_cols, 0)
    swapped = pairwise(cut(tile, (1 - core) * tile_cols, tile_cols, 0), "col", 0, "swap")
    most = tile_cols // 2
    pieces = [mine[:most], swapped[:most], mine[most:], swapped[most:]]
    hops, got = [], []

    ends = [tile[:, 0], tile[:, tile_cols - 1]]
    near = pairwise(jnp.where(core == 0, ends[1], ends[0]), "col", 0, "own_near")
    far = pairwise(jnp.where(core == 0, ends[0], ends[1]), "col", 1, "own_far")
    before, after = sides(near, far)
    ends = [
        jnp.concatenate([before[y : y + 1], tile[y], after[y : y + 1]]) for y in (0, tile_rows - 1)
    ]
    band_near = pairwise(jnp.where(up == 0, ends[1], ends[0]), "row", 0, "own_band_near")
    band_far = pairwise(jnp.where(up == 0, ends[0], ends[1]), "row", 1, "own_band_far")
    band_near, band_far, *pieces = lax.optimization_barrier((band_near, band_far, *pieces))
    for i, piece in enumerate(pieces):
        with jax.named_scope(f"hop{i}"):
            hops.append(place.hop(piece, i % 2))
    for i, hop in enumerate(hops):
        with jax.named_scope(f"land{i}"):
            got.append(place.land(hop, i % 2))
    first, ring, other_ring = call(
        "first",
        lambda *refs: first_kernel(*refs, step=divisor(tile_rows, 16)),
        (shape(tile_rows, tile_cols), *(shape(3 * tile_cols),) * 2),
        (tile, near, far, band_near, band_far, w_first),
        [
            scratch(tile_rows + 2, tile_cols + 2 * PAD, channels),
            scratch(tile_rows + 2, tile_cols, 3 * channels),
        ],
        tile_rows * tile_cols,
    )
    ring = jnp.concatenate([ring, pairwise(other_ring, "col", 0, "ring_swap")])
    with jax.named_scope("ring"):
        got_ring = place.direct(ring)
    (turned,) = call(
        "turned",
        lambda *refs: turned_kernel(*refs, step=divisor(tile_cols, 8)),
        (shape(tile_cols, tile_rows),),
        (*pieces, *got, w_first),
        [
            scratch(tile_cols + 2, tile_rows + 2 * PAD, channels),
            scratch(tile_cols + 2, tile_rows, 3 * channels),
        ],
        tile_rows * tile_cols,
    )
    sym, to_near, to_far = call(
        "mean",
        mean_kernel,
        (shape(tile_rows, tile_cols), shape(tile_rows, STRIP), shape(tile_rows, STRIP)),
        (first, turned, ring, got_ring),
        [scratch(tile_cols, tile_rows, channels), scratch(6 * tile_cols, channels)],
    )

    near = pairwise(to_near, "col", 0, "sym_near")
    far = pairwise(to_far, "col", 1, "sym_far")
    rows2, rows3 = tile_rows - 4, tile_rows - 2 * EDGE
    (inner,) = call(
        "inner_second",
        lambda *refs: inner_second_kernel(*refs, step=divisor(rows2, 20)),
        (shape(rows2, tile_cols),),
        (sym, w_second),
        [scratch(tile_rows, tile_cols, 3 * channels)],
        2 * rows2 * tile_cols,
    )
    before, after = sides(near, far)

    def band(at):
        return jnp.concatenate([cut(part, at, HALO, 0) for part in (before, sym, after)], axis=1)

    last = tile_rows - HALO
    band_near = pairwise(band((1 - up) * last), "row", 0, "sym_band_near")
    band_far = pairwise(band(up * last), "row", 1, "sym_band_far")
    width = tile_cols + 2 * STRIP
    step = divisor(rows3, 26)
    features, tops, bottoms = call(
        "middle",
        lambda *refs: middle_kernel(*refs, steps=(divisor(rows2, 30), step)),
        (shape(tile_rows, tile_cols), shape(STRIP, width), shape(STRIP, width)),
        (sym, near, far, inner, w_second, w_third),
        [
            scratch(tile_rows, tile_cols + 2 * PAD, channels),
            scratch(tile_rows, 16, 3 * channels),
            scratch(rows2, width, channels),
            scratch(rows2, tile_cols, 3 * channels),
            scratch(rows3, tile_cols, channels),
            pltpu.SemaphoreType.DMA((rows3 // step,)),
        ],
        2 * rows2 * 16 + rows3 * tile_cols,
        out_specs=(anywhere, *whole(2)),
    )
    return call(
        "edges",
        edges_kernel,
        (shape(tile_rows, tile_cols),),
        (features, sym, near, far, band_near, band_far, tops, bottoms, w_second, w_third),
        [
            scratch(2, HALO + 4, tile_cols + 2 * PAD, channels),
            scratch(2, HALO + 4, width, 3 * channels),
            scratch(2, HALO + STRIP, width, channels),
            scratch(2, HALO + STRIP, tile_cols, 3 * channels),
            scratch(2, EDGE, tile_cols, channels),
            pltpu.SemaphoreType.DMA((2,)),
        ],
        2 * 2 * HALO * width + 2 * EDGE * tile_cols,
        in_specs=[anywhere] + whole(9),
        out_specs=(anywhere,),
        alias={0: 0},
    )[0]


def solution(mesh):
    return jax.shard_map(
        local,
        mesh=mesh,
        in_specs=(P("row", "col", None), P(), P(), P()),
        out_specs=P("row", "col", None),
        check_vma=False,
    )
```

```python
import math

import jax
import jax.numpy as jnp
import numpy as np
from jax import lax
from jax.experimental import pallas as pl
from jax.experimental.pallas import tpu as pltpu
from jax.sharding import PartitionSpec as P

AXES = ("row", "col")
BF16, F32 = jnp.bfloat16, jnp.float32
PAD = 16
STRIP = 8
HALO = 6
EDGE = 6


def routes(row_count, plan):
    low = math.isqrt(row_count)
    first, second = {}, {}
    for r in range(row_count):
        for z in range(row_count):
            a, b, c, d = r // low, r % low, z // low, z % low
            if r == z:
                continue
            straight, across = (b == d, a == c) if plan == 0 else (a == c, b == d)
            turn = c * low + b if plan == 0 else a * low + d
            via = (r if straight else z if across else turn, z)
            first[(r, z)] = via
            second.setdefault(via, []).append((z, r))
    if any(len(ends) > 1 for ends in second.values()) or len(set(first.values())) < len(first):
        return {}, {(r, z): (z, r) for r in range(row_count) for z in range(row_count) if r != z}
    return first, {via: ends[0] for via, ends in second.items()}


class Place:
    def __init__(self):
        self.rows, self.cols = lax.axis_size("row"), lax.axis_size("col")
        self.row, self.col = lax.axis_index("row"), lax.axis_index("col")
        self.core = self.col % 2
        self.up = self.row % 2
        self.diagonal = self.row == self.col // 2
        self.legs = [routes(self.rows, plan) for plan in range(2)]

    def chips(self, array, legs):
        pairs = [
            (s[0] * self.cols + s[1] * 2 + k, e[0] * self.cols + e[1] * 2 + k)
            for s, e in legs.items()
            for k in range(2)
        ]
        return lax.ppermute(array, AXES, pairs)

    def hop(self, piece, plan):
        first = self.legs[plan][0]
        return self.chips(piece, first) if first else piece

    def direct(self, piece):
        places = [(r, z) for r in range(self.rows) for z in range(self.rows) if r != z]
        return self.chips(piece, {(r, z): (z, r) for r, z in places})

    def land(self, hopped, plan):
        return self.chips(hopped, self.legs[plan][1])


def pairwise(array, axis, start, name):
    size = lax.axis_size(axis)
    pairs = [(i, i + 1) for i in range(start, size - 1, 2)]
    if not pairs:
        return jnp.zeros_like(array)
    with jax.named_scope(name):
        return lax.ppermute(array, axis, pairs + [(j, i) for i, j in pairs])


def widen(wide, padded, start, width, step):
    channels = padded.shape[2]
    for q in range(3):
        at = start + q * step
        wide[:, :, q * channels : (q + 1) * channels] = padded[:, at : at + width, :]


def products(wide, weight, row, rows, step, flip=False):
    width, channels = wide.shape[1], wide.shape[2] // 3
    taps = [
        wide[pl.ds(row + p * step, rows), :, q * channels : (q + 1) * channels].reshape(
            rows * width, channels
        )
        for p in range(3)
        for q in range(3)
    ]
    if flip:
        taps = [taps[q * 3 + p] for p in range(3) for q in range(3)]
    flat = weight[...].reshape(9 * channels, weight.shape[3])
    return jnp.maximum(jnp.dot(jnp.concatenate(taps, axis=1), flat, preferred_element_type=F32), 0.0)


def sides(near, far):
    core = lax.axis_index("col") % 2
    return jnp.where(core == 0, far, near), jnp.where(core == 0, near, far)


def put_tile(padded, tile, near, far):
    rows, cols, channels = tile.shape
    padded[1 : 1 + rows, PAD : PAD + cols, :] = tile[...]
    before, after = sides(near[...], far[...])
    padded[1 : 1 + rows, PAD - 1 : PAD, :] = before.reshape(rows, 1, channels)
    padded[1 : 1 + rows, PAD + cols : PAD + cols + 1, :] = after.reshape(rows, 1, channels)


def first_kernel(tile, near, far, band_near, band_far, weight, out, mine, other, padded, wide, *, step):
    core, up = lax.axis_index("col") % 2, lax.axis_index("row") % 2
    rows, cols, channels = tile.shape
    put_tile(padded, tile, near, far)
    ends = slice(PAD - 1, PAD + cols + 1)
    padded[0, ends, :] = jnp.where(up == 0, band_far[...], band_near[...])
    padded[rows + 1, ends, :] = jnp.where(up == 0, band_near[...], band_far[...])
    widen(wide, padded, PAD - 1, cols, 1)
    for at in range(0, rows, step):
        value = products(wide, weight, at, step, 1)
        out[at : at + step] = value.astype(BF16).reshape(step, cols, channels)
    outer = jnp.where(core == 0, out[:, 0, :], out[:, cols - 1, :])
    for half in range(2):
        top = half * cols

        def put(ring, top=top):
            ring[:cols] = out[top]
            ring[cols : 2 * cols] = out[top + cols - 1]
            ring[2 * cols :] = outer[top : top + cols]

        pl.when(core == half)(lambda put=put: put(mine))
        pl.when(core != half)(lambda put=put: put(other))


def turned_kernel(kept0, kept1, kept2, kept3, got0, got1, got2, got3, weight, out, padded, wide, *, step):
    core = lax.axis_index("col") % 2
    diagonal = lax.axis_index("row") == lax.axis_index("col") // 2
    size, length, channels = out.shape
    rows = kept0.shape[0]

    def put(pieces):
        for side in range(2):
            left = PAD + side * size

            def fill(first, second, left=left):
                padded[1 : 1 + rows, left : left + size, :] = first[...]
                padded[1 + rows : 1 + size, left : left + size, :] = second[...]

            pl.when(core == side)(lambda fill=fill: fill(pieces[0], pieces[2]))
            pl.when(core != side)(lambda fill=fill: fill(pieces[1], pieces[3]))

    pl.when(diagonal)(lambda: put((kept0, kept1, kept2, kept3)))
    pl.when(jnp.logical_not(diagonal))(lambda: put((got0, got1, got2, got3)))
    widen(wide, padded, PAD - 1, length, 1)
    for at in range(0, size, step):
        value = products(wide, weight, at, step, 1)
        out[at : at + step] = value.astype(BF16).reshape(step, length, channels)


def mean_kernel(first, turned, kept, got, out, to_near, to_far, block, ring):
    row, col = lax.axis_index("row"), lax.axis_index("col")
    core = col % 2
    diagonal = row == col // 2
    size, length, channels = turned.shape
    count = 3 * size
    ring[...] = jnp.where(diagonal, kept[...], got[...])
    block[...] = turned[...]
    for side in range(2):
        left = side * size
        edge = 0 if side == 0 else length - 1

        def put(at, left=left, edge=edge):
            block[0, left : left + size, :] = ring[at : at + size]
            block[size - 1, left : left + size, :] = ring[at + size : at + 2 * size]
            outer = ring[at + 2 * size : at + count]
            block[:, edge : edge + 1, :] = outer.reshape(size, 1, channels)

        pl.when(core == side)(lambda put=put: put(0))
        pl.when(core != side)(lambda put=put: put(count))
    for side in range(2):
        rows = slice(side * size, (side + 1) * size)
        other = jnp.swapaxes(block[:, rows, :], 0, 1).astype(F32)
        out[rows] = ((first[rows].astype(F32) + other) * 0.5).astype(BF16)
    start, end = out[:, :STRIP, :], out[:, size - STRIP :, :]
    to_near[...] = jnp.where(core == 0, end, start)
    to_far[...] = jnp.where(core == 0, start, end)


def second_rows(wide, weight, at, rows, valid):
    a = products(wide, weight, at, rows, 2).astype(BF16).astype(F32)
    b = products(wide, weight, at, rows, 2, flip=True).astype(BF16).astype(F32)
    mean = ((a + b) * 0.5).reshape(rows, wide.shape[1], -1)
    return jnp.where(valid, mean, 0.0).astype(BF16)


def columns_inside(x, tile_cols):
    x = x + lax.axis_index("col") * tile_cols
    return (x >= 0) & (x < tile_cols * lax.axis_size("col"))


def inner_second_kernel(sym, weight, out, wide, *, step):
    cols, channels = sym.shape[1], sym.shape[2]
    wide[:, 2:, :channels] = sym[:, : cols - 2, :]
    wide[:, :, channels : 2 * channels] = sym[...]
    wide[:, : cols - 2, 2 * channels :] = sym[:, 2:, :]
    for at in range(0, out.shape[0], step):
        out[at : at + step] = second_rows(wide, weight, at, step, True)


def middle_kernel(
    sym, near, far, inner, w_second, w_third, features, tops, bottoms, padded, wide2, sym2, wide3, out, done,
    *, steps
):
    tile_rows, tile_cols, channels = sym.shape
    end = PAD + tile_cols
    padded[:, PAD:end, :] = sym[...]
    before, after = sides(near[...], far[...])
    padded[:, PAD - STRIP : PAD, :] = before
    padded[:, end : end + STRIP, :] = after
    half = wide2.shape[1] // 2
    for q in range(3):
        lanes = slice(q * channels, (q + 1) * channels)
        at = PAD - 6 + 2 * q
        wide2[:, :half, lanes] = padded[:, at : at + half, :]
        at += tile_cols
        wide2[:, half:, lanes] = padded[:, at : at + half, :]
    x = lax.broadcasted_iota(jnp.int32, (1, 2 * half, 1), 1)
    valid = columns_inside(jnp.where(x < half, x - 4, x - half + tile_cols - 4), tile_cols)
    rows2, rows3 = sym2.shape[0], out.shape[0]
    sym2[:, STRIP : STRIP + tile_cols, :] = inner[...]
    for at in range(0, rows2, steps[0]):
        value = second_rows(wide2, w_second, at, steps[0], valid)
        rows = slice(at, at + steps[0])
        sym2[rows, STRIP - 4 : STRIP - 4 + half, :] = value[:, :half, :]
        to = STRIP + tile_cols - 4
        sym2[rows, to : to + half, :] = value[:, half:, :]
    tops[...] = sym2[0:STRIP]
    bottoms[...] = sym2[rows2 - STRIP : rows2]
    widen(wide3, sym2, STRIP - 4, tile_cols, 4)
    copies = []
    for i, at in enumerate(range(0, rows3, steps[1])):
        value = products(wide3, w_third, at, steps[1], 4)
        rows = pl.ds(at, steps[1])
        out[rows] = value.astype(BF16).reshape(steps[1], tile_cols, channels)
        target = features.at[pl.ds(EDGE + at, steps[1])]
        copies.append(pltpu.make_async_copy(out.at[rows], target, done.at[i]))
        copies[-1].start()
    for copy in copies:
        copy.wait()


def edges_kernel(
    _, sym, near, far, band_near, band_far, tops, bottoms, w_second, w_third, features,
    padded, wide2, sym2, wide3, out, done,
):
    row = lax.axis_index("row")
    up = row % 2
    tile_rows, tile_cols, channels = sym.shape
    end = PAD + tile_cols
    width = wide2.shape[2]
    side = (width - tile_cols) // 2
    x = lax.broadcasted_iota(jnp.int32, (1, width, 1), 1) - side
    valid = columns_inside(x, tile_cols)
    rows = padded.shape[1] - HALO
    bands = (
        jnp.where(up == 0, band_far[...], band_near[...]),
        jnp.where(up == 0, band_near[...], band_far[...]),
    )
    targets = [features.at[pl.ds(0, EDGE)], features.at[pl.ds(tile_rows - EDGE, EDGE)]]
    copies = [pltpu.make_async_copy(out.at[i], targets[i], done.at[i]) for i in range(2)]
    y = lax.broadcasted_iota(jnp.int32, (HALO, 1, 1), 0)
    insides = [
        row * tile_rows - 4 + y >= 0,
        (row + 1) * tile_rows - 2 + y < tile_rows * lax.axis_size("row"),
    ]
    for i in range(2):
        own = slice(HALO, HALO + rows) if i == 0 else slice(0, rows)
        outside = slice(0, HALO) if i == 0 else slice(rows, rows + HALO)
        source = slice(0, rows) if i == 0 else slice(tile_rows - rows, tile_rows)
        padded[i, own, PAD:end, :] = sym[source]
        before, after = sides(near[source], far[source])
        padded[i, own, PAD - STRIP : PAD, :] = before
        padded[i, own, end : end + STRIP, :] = after
        padded[i, outside, PAD - STRIP : end + STRIP, :] = bands[i]
        widen(wide2.at[i], padded.at[i], PAD - side - 2, width, 2)
    values = [second_rows(wide2.at[i], w_second, 0, HALO, valid & insides[i]) for i in range(2)]
    sym2[0, 0:HALO], sym2[0, HALO:] = values[0], tops[...]
    sym2[1, 0:STRIP], sym2[1, STRIP:] = bottoms[...], values[1]
    for i in range(2):
        widen(wide3.at[i], sym2.at[i], side - 4, tile_cols, 4)
    for i in range(2):
        value = products(wide3.at[i], w_third, 0, EDGE, 4)
        out[i] = value.astype(BF16).reshape(EDGE, tile_cols, channels)
        copies[i].start()
    for copy in copies:
        copy.wait()


def whole(count):
    return [pl.BlockSpec(memory_space=pltpu.VMEM)] * count


def divisor(number, most):
    return max(d for d in range(1, most + 1) if number % d == 0)


def cut(array, at, size, dim):
    return lax.dynamic_slice_in_dim(array, at, size, dim)


def local(contacts, w_first, w_second, w_third):
    tile_rows, tile_cols, channels = contacts.shape
    place = Place()
    core, up = place.core, place.up
    anywhere = pl.BlockSpec(memory_space=pl.ANY)

    def shape(*dims):
        return jax.ShapeDtypeStruct((*dims, channels), BF16)

    def scratch(*dims):
        return pltpu.VMEM(dims, BF16)

    def call(name, kernel, outs, ins, scratches, pixels=0, in_specs=None, out_specs=None, alias=None):
        macs = pixels * 9 * channels * channels
        return pl.pallas_call(
            kernel,
            out_shape=outs,
            in_specs=in_specs or whole(len(ins)),
            out_specs=out_specs or tuple(whole(len(outs))),
            scratch_shapes=scratches,
            input_output_aliases=alias or {},
            compiler_params=pltpu.CompilerParams(vmem_limit_bytes=24 * 2**20),
            cost_estimate=pl.CostEstimate(
                flops=2 * macs, bytes_accessed=18 * channels * channels, transcendentals=0
            ),
            name=name,
        )(*ins)

    tile = contacts
    mine = cut(tile, core * tile_cols, tile_cols, 0)
    swapped = pairwise(cut(tile, (1 - core) * tile_cols, tile_cols, 0), "col", 0, "swap")
    most = tile_cols // 2
    pieces = [mine[:most], swapped[:most], mine[most:], swapped[most:]]
    hops, got = [], []

    ends = [tile[:, 0], tile[:, tile_cols - 1]]
    near = pairwise(jnp.where(core == 0, ends[1], ends[0]), "col", 0, "own_near")
    far = pairwise(jnp.where(core == 0, ends[0], ends[1]), "col", 1, "own_far")
    before, after = sides(near, far)
    ends = [
        jnp.concatenate([before[y : y + 1], tile[y], after[y : y + 1]]) for y in (0, tile_rows - 1)
    ]
    band_near = pairwise(jnp.where(up == 0, ends[1], ends[0]), "row", 0, "own_band_near")
    band_far = pairwise(jnp.where(up == 0, ends[0], ends[1]), "row", 1, "own_band_far")
    band_near, band_far, *pieces = lax.optimization_barrier((band_near, band_far, *pieces))
    for i, piece in enumerate(pieces):
        with jax.named_scope(f"hop{i}"):
            hops.append(place.hop(piece, (0, 1, 1, 0)[i]))
    for i, hop in enumerate(hops):
        with jax.named_scope(f"land{i}"):
            got.append(place.land(hop, (0, 1, 1, 0)[i]))
    first, ring, other_ring = call(
        "first",
        lambda *refs: first_kernel(*refs, step=divisor(tile_rows, 16)),
        (shape(tile_rows, tile_cols), *(shape(3 * tile_cols),) * 2),
        (tile, near, far, band_near, band_far, w_first),
        [
            scratch(tile_rows + 2, tile_cols + 2 * PAD, channels),
            scratch(tile_rows + 2, tile_cols, 3 * channels),
        ],
        tile_rows * tile_cols,
    )
    ring = jnp.concatenate([ring, pairwise(other_ring, "col", 0, "ring_swap")])
    with jax.named_scope("ring"):
        got_ring = place.direct(ring)
    (turned,) = call(
        "turned",
        lambda *refs: turned_kernel(*refs, step=divisor(tile_cols, 8)),
        (shape(tile_cols, tile_rows),),
        (*pieces, *got, w_first),
        [
            scratch(tile_cols + 2, tile_rows + 2 * PAD, channels),
            scratch(tile_cols + 2, tile_rows, 3 * channels),
        ],
        tile_rows * tile_cols,
    )
    sym, to_near, to_far = call(
        "mean",
        mean_kernel,
        (shape(tile_rows, tile_cols), shape(tile_rows, STRIP), shape(tile_rows, STRIP)),
        (first, turned, ring, got_ring),
        [scratch(tile_cols, tile_rows, channels), scratch(6 * tile_cols, channels)],
    )

    near = pairwise(to_near, "col", 0, "sym_near")
    far = pairwise(to_far, "col", 1, "sym_far")
    rows2, rows3 = tile_rows - 4, tile_rows - 2 * EDGE
    (inner,) = call(
        "inner_second",
        lambda *refs: inner_second_kernel(*refs, step=divisor(rows2, 20)),
        (shape(rows2, tile_cols),),
        (sym, w_second),
        [scratch(tile_rows, tile_cols, 3 * channels)],
        2 * rows2 * tile_cols,
    )
    before, after = sides(near, far)

    def band(at):
        return jnp.concatenate([cut(part, at, HALO, 0) for part in (before, sym, after)], axis=1)

    last = tile_rows - HALO
    band_near = pairwise(band((1 - up) * last), "row", 0, "sym_band_near")
    band_far = pairwise(band(up * last), "row", 1, "sym_band_far")
    width = tile_cols + 2 * STRIP
    step = divisor(rows3, 26)
    features, tops, bottoms = call(
        "middle",
        lambda *refs: middle_kernel(*refs, steps=(divisor(rows2, 30), step)),
        (shape(tile_rows, tile_cols), shape(STRIP, width), shape(STRIP, width)),
        (sym, near, far, inner, w_second, w_third),
        [
            scratch(tile_rows, tile_cols + 2 * PAD, channels),
            scratch(tile_rows, 16, 3 * channels),
            scratch(rows2, width, channels),
            scratch(rows2, tile_cols, 3 * channels),
            scratch(rows3, tile_cols, channels),
            pltpu.SemaphoreType.DMA((rows3 // step,)),
        ],
        2 * rows2 * 16 + rows3 * tile_cols,
        out_specs=(anywhere, *whole(2)),
    )
    return call(
        "edges",
        edges_kernel,
        (shape(tile_rows, tile_cols),),
        (features, sym, near, far, band_near, band_far, tops, bottoms, w_second, w_third),
        [
            scratch(2, HALO + 4, tile_cols + 2 * PAD, channels),
            scratch(2, HALO + 4, width, 3 * channels),
            scratch(2, HALO + STRIP, width, channels),
            scratch(2, HALO + STRIP, tile_cols, 3 * channels),
            scratch(2, EDGE, tile_cols, channels),
            pltpu.SemaphoreType.DMA((2,)),
        ],
        2 * 2 * HALO * width + 2 * EDGE * tile_cols,
        in_specs=[anywhere] + whole(9),
        out_specs=(anywhere,),
        alias={0: 0},
    )[0]


def solution(mesh):
    return jax.shard_map(
        local,
        mesh=mesh,
        in_specs=(P("row", "col", None), P(), P(), P()),
        out_specs=P("row", "col", None),
        check_vma=False,
    )
```

```python
import math

import jax
import jax.numpy as jnp
import numpy as np
from jax import lax
from jax.experimental import pallas as pl
from jax.experimental.pallas import tpu as pltpu
from jax.sharding import PartitionSpec as P

AXES = ("row", "col")
BF16, F32 = jnp.bfloat16, jnp.float32
PAD = 16
STRIP = 8
HALO = 6
EDGE = 6


def routes(row_count, plan):
    low = math.isqrt(row_count)
    first, second = {}, {}
    for r in range(row_count):
        for z in range(row_count):
            a, b, c, d = r // low, r % low, z // low, z % low
            if r == z:
                continue
            straight, across = (b == d, a == c) if plan == 0 else (a == c, b == d)
            turn = c * low + b if plan == 0 else a * low + d
            via = (r if straight else z if across else turn, z)
            first[(r, z)] = via
            second.setdefault(via, []).append((z, r))
    if any(len(ends) > 1 for ends in second.values()) or len(set(first.values())) < len(first):
        return {}, {(r, z): (z, r) for r in range(row_count) for z in range(row_count) if r != z}
    return first, {via: ends[0] for via, ends in second.items()}


class Place:
    def __init__(self):
        self.rows, self.cols = lax.axis_size("row"), lax.axis_size("col")
        self.row, self.col = lax.axis_index("row"), lax.axis_index("col")
        self.core = self.col % 2
        self.up = self.row % 2
        self.diagonal = self.row == self.col // 2
        self.legs = [routes(self.rows, plan) for plan in range(2)]

    def chips(self, array, legs):
        pairs = [
            (s[0] * self.cols + s[1] * 2 + k, e[0] * self.cols + e[1] * 2 + k)
            for s, e in legs.items()
            for k in range(2)
        ]
        return lax.ppermute(array, AXES, pairs)

    def hop(self, piece, plan):
        first = self.legs[plan][0]
        return self.chips(piece, first) if first else piece

    def direct(self, piece):
        places = [(r, z) for r in range(self.rows) for z in range(self.rows) if r != z]
        return self.chips(piece, {(r, z): (z, r) for r, z in places})

    def land(self, hopped, plan):
        return self.chips(hopped, self.legs[plan][1])


def pairwise(array, axis, start, name):
    size = lax.axis_size(axis)
    pairs = [(i, i + 1) for i in range(start, size - 1, 2)]
    if not pairs:
        return jnp.zeros_like(array)
    with jax.named_scope(name):
        return lax.ppermute(array, axis, pairs + [(j, i) for i, j in pairs])


def widen(wide, padded, start, width, step):
    channels = padded.shape[2]
    for q in range(3):
        at = start + q * step
        wide[:, :, q * channels : (q + 1) * channels] = padded[:, at : at + width, :]


def products(wide, weight, row, rows, step, flip=False):
    width, channels = wide.shape[1], wide.shape[2] // 3
    taps = [
        wide[pl.ds(row + p * step, rows), :, q * channels : (q + 1) * channels].reshape(
            rows * width, channels
        )
        for p in range(3)
        for q in range(3)
    ]
    if flip:
        taps = [taps[q * 3 + p] for p in range(3) for q in range(3)]
    flat = weight[...].reshape(9 * channels, weight.shape[3])
    return jnp.maximum(jnp.dot(jnp.concatenate(taps, axis=1), flat, preferred_element_type=F32), 0.0)


def sides(near, far):
    core = lax.axis_index("col") % 2
    return jnp.where(core == 0, far, near), jnp.where(core == 0, near, far)


def put_tile(padded, tile, near, far):
    rows, cols, channels = tile.shape
    padded[1 : 1 + rows, PAD : PAD + cols, :] = tile[...]
    before, after = sides(near[...], far[...])
    padded[1 : 1 + rows, PAD - 1 : PAD, :] = before.reshape(rows, 1, channels)
    padded[1 : 1 + rows, PAD + cols : PAD + cols + 1, :] = after.reshape(rows, 1, channels)


def first_kernel(tile, near, far, band_near, band_far, weight, out, mine, other, padded, wide, *, step):
    core, up = lax.axis_index("col") % 2, lax.axis_index("row") % 2
    rows, cols, channels = tile.shape
    put_tile(padded, tile, near, far)
    ends = slice(PAD - 1, PAD + cols + 1)
    padded[0, ends, :] = jnp.where(up == 0, band_far[...], band_near[...])
    padded[rows + 1, ends, :] = jnp.where(up == 0, band_near[...], band_far[...])
    widen(wide, padded, PAD - 1, cols, 1)
    for at in range(0, rows, step):
        value = products(wide, weight, at, step, 1)
        out[at : at + step] = value.astype(BF16).reshape(step, cols, channels)
    outer = jnp.where(core == 0, out[:, 0, :], out[:, cols - 1, :])
    for half in range(2):
        top = half * cols

        def put(ring, top=top):
            ring[:cols] = out[top]
            ring[cols : 2 * cols] = out[top + cols - 1]
            ring[2 * cols :] = outer[top : top + cols]

        pl.when(core == half)(lambda put=put: put(mine))
        pl.when(core != half)(lambda put=put: put(other))


def turned_kernel(kept0, kept1, kept2, kept3, got0, got1, got2, got3, weight, out, padded, wide, *, step):
    core = lax.axis_index("col") % 2
    diagonal = lax.axis_index("row") == lax.axis_index("col") // 2
    size, length, channels = out.shape
    rows = kept0.shape[0]

    def put(pieces):
        for side in range(2):
            left = PAD + side * size

            def fill(first, second, left=left):
                padded[1 : 1 + rows, left : left + size, :] = first[...]
                padded[1 + rows : 1 + size, left : left + size, :] = second[...]

            pl.when(core == side)(lambda fill=fill: fill(pieces[0], pieces[2]))
            pl.when(core != side)(lambda fill=fill: fill(pieces[1], pieces[3]))

    pl.when(diagonal)(lambda: put((kept0, kept1, kept2, kept3)))
    pl.when(jnp.logical_not(diagonal))(lambda: put((got0, got1, got2, got3)))
    widen(wide, padded, PAD - 1, length, 1)
    for at in range(0, size, step):
        value = products(wide, weight, at, step, 1)
        out[at : at + step] = value.astype(BF16).reshape(step, length, channels)


def mean_kernel(first, turned, kept, got, out, to_near, to_far, block, ring):
    row, col = lax.axis_index("row"), lax.axis_index("col")
    core = col % 2
    diagonal = row == col // 2
    size, length, channels = turned.shape
    count = 3 * size
    ring[...] = jnp.where(diagonal, kept[...], got[...])
    block[...] = turned[...]
    for side in range(2):
        left = side * size
        edge = 0 if side == 0 else length - 1

        def put(at, left=left, edge=edge):
            block[0, left : left + size, :] = ring[at : at + size]
            block[size - 1, left : left + size, :] = ring[at + size : at + 2 * size]
            outer = ring[at + 2 * size : at + count]
            block[:, edge : edge + 1, :] = outer.reshape(size, 1, channels)

        pl.when(core == side)(lambda put=put: put(0))
        pl.when(core != side)(lambda put=put: put(count))
    for side in range(2):
        rows = slice(side * size, (side + 1) * size)
        other = jnp.swapaxes(block[:, rows, :], 0, 1).astype(F32)
        out[rows] = ((first[rows].astype(F32) + other) * 0.5).astype(BF16)
    start, end = out[:, :STRIP, :], out[:, size - STRIP :, :]
    to_near[...] = jnp.where(core == 0, end, start)
    to_far[...] = jnp.where(core == 0, start, end)


def second_rows(wide, weight, at, rows, valid):
    a = products(wide, weight, at, rows, 2).astype(BF16).astype(F32)
    b = products(wide, weight, at, rows, 2, flip=True).astype(BF16).astype(F32)
    mean = ((a + b) * 0.5).reshape(rows, wide.shape[1], -1)
    return jnp.where(valid, mean, 0.0).astype(BF16)


def columns_inside(x, tile_cols):
    x = x + lax.axis_index("col") * tile_cols
    return (x >= 0) & (x < tile_cols * lax.axis_size("col"))


def inner_second_kernel(sym, weight, out, wide, *, step):
    cols, channels = sym.shape[1], sym.shape[2]
    wide[:, 2:, :channels] = sym[:, : cols - 2, :]
    wide[:, :, channels : 2 * channels] = sym[...]
    wide[:, : cols - 2, 2 * channels :] = sym[:, 2:, :]
    for at in range(0, out.shape[0], step):
        out[at : at + step] = second_rows(wide, weight, at, step, True)


def middle_kernel(
    sym, near, far, inner, w_second, w_third, features, tops, bottoms, padded, wide2, sym2, wide3, out, done,
    *, steps
):
    tile_rows, tile_cols, channels = sym.shape
    end = PAD + tile_cols
    padded[:, PAD:end, :] = sym[...]
    before, after = sides(near[...], far[...])
    padded[:, PAD - STRIP : PAD, :] = before
    padded[:, end : end + STRIP, :] = after
    half = wide2.shape[1] // 2
    for q in range(3):
        lanes = slice(q * channels, (q + 1) * channels)
        at = PAD - 6 + 2 * q
        wide2[:, :half, lanes] = padded[:, at : at + half, :]
        at += tile_cols
        wide2[:, half:, lanes] = padded[:, at : at + half, :]
    x = lax.broadcasted_iota(jnp.int32, (1, 2 * half, 1), 1)
    valid = columns_inside(jnp.where(x < half, x - 4, x - half + tile_cols - 4), tile_cols)
    rows2, rows3 = sym2.shape[0], out.shape[0]
    sym2[:, STRIP : STRIP + tile_cols, :] = inner[...]
    for at in range(0, rows2, steps[0]):
        value = second_rows(wide2, w_second, at, steps[0], valid)
        rows = slice(at, at + steps[0])
        sym2[rows, STRIP - 4 : STRIP - 4 + half, :] = value[:, :half, :]
        to = STRIP + tile_cols - 4
        sym2[rows, to : to + half, :] = value[:, half:, :]
    tops[...] = sym2[0:STRIP]
    bottoms[...] = sym2[rows2 - STRIP : rows2]
    widen(wide3, sym2, STRIP - 4, tile_cols, 4)
    copies = []
    for i, at in enumerate(range(0, rows3, steps[1])):
        value = products(wide3, w_third, at, steps[1], 4)
        rows = pl.ds(at, steps[1])
        out[rows] = value.astype(BF16).reshape(steps[1], tile_cols, channels)
        target = features.at[pl.ds(EDGE + at, steps[1])]
        copies.append(pltpu.make_async_copy(out.at[rows], target, done.at[i]))
        copies[-1].start()
    for copy in copies:
        copy.wait()


def edges_kernel(
    _, sym, near, far, band_near, band_far, tops, bottoms, w_second, w_third, features,
    padded, wide2, sym2, wide3, out, done,
):
    row = lax.axis_index("row")
    up = row % 2
    tile_rows, tile_cols, channels = sym.shape
    end = PAD + tile_cols
    width = wide2.shape[2]
    side = (width - tile_cols) // 2
    x = lax.broadcasted_iota(jnp.int32, (1, width, 1), 1) - side
    valid = columns_inside(x, tile_cols)
    rows = padded.shape[1] - HALO
    bands = (
        jnp.where(up == 0, band_far[...], band_near[...]),
        jnp.where(up == 0, band_near[...], band_far[...]),
    )
    targets = [features.at[pl.ds(0, EDGE)], features.at[pl.ds(tile_rows - EDGE, EDGE)]]
    copies = [pltpu.make_async_copy(out.at[i], targets[i], done.at[i]) for i in range(2)]
    y = lax.broadcasted_iota(jnp.int32, (HALO, 1, 1), 0)
    insides = [
        row * tile_rows - 4 + y >= 0,
        (row + 1) * tile_rows - 2 + y < tile_rows * lax.axis_size("row"),
    ]
    for i in range(2):
        own = slice(HALO, HALO + rows) if i == 0 else slice(0, rows)
        outside = slice(0, HALO) if i == 0 else slice(rows, rows + HALO)
        source = slice(0, rows) if i == 0 else slice(tile_rows - rows, tile_rows)
        padded[i, own, PAD:end, :] = sym[source]
        before, after = sides(near[source], far[source])
        padded[i, own, PAD - STRIP : PAD, :] = before
        padded[i, own, end : end + STRIP, :] = after
        padded[i, outside, PAD - STRIP : end + STRIP, :] = bands[i]
        widen(wide2.at[i], padded.at[i], PAD - side - 2, width, 2)
    values = [second_rows(wide2.at[i], w_second, 0, HALO, valid & insides[i]) for i in range(2)]
    sym2[0, 0:HALO], sym2[0, HALO:] = values[0], tops[...]
    sym2[1, 0:STRIP], sym2[1, STRIP:] = bottoms[...], values[1]
    for i in range(2):
        widen(wide3.at[i], sym2.at[i], side - 4, tile_cols, 4)
    for i in range(2):
        value = products(wide3.at[i], w_third, 0, EDGE, 4)
        out[i] = value.astype(BF16).reshape(EDGE, tile_cols, channels)
        copies[i].start()
    for copy in copies:
        copy.wait()


def whole(count):
    return [pl.BlockSpec(memory_space=pltpu.VMEM)] * count


def divisor(number, most):
    return max(d for d in range(1, most + 1) if number % d == 0)


def cut(array, at, size, dim):
    return lax.dynamic_slice_in_dim(array, at, size, dim)


def local(contacts, w_first, w_second, w_third):
    tile_rows, tile_cols, channels = contacts.shape
    place = Place()
    core, up = place.core, place.up
    anywhere = pl.BlockSpec(memory_space=pl.ANY)

    def shape(*dims):
        return jax.ShapeDtypeStruct((*dims, channels), BF16)

    def scratch(*dims):
        return pltpu.VMEM(dims, BF16)

    def call(name, kernel, outs, ins, scratches, pixels=0, in_specs=None, out_specs=None, alias=None):
        macs = pixels * 9 * channels * channels
        return pl.pallas_call(
            kernel,
            out_shape=outs,
            in_specs=in_specs or whole(len(ins)),
            out_specs=out_specs or tuple(whole(len(outs))),
            scratch_shapes=scratches,
            input_output_aliases=alias or {},
            compiler_params=pltpu.CompilerParams(vmem_limit_bytes=24 * 2**20),
            cost_estimate=pl.CostEstimate(
                flops=2 * macs, bytes_accessed=18 * channels * channels, transcendentals=0
            ),
            name=name,
        )(*ins)

    tile = contacts
    mine = cut(tile, core * tile_cols, tile_cols, 0)
    swapped = pairwise(cut(tile, (1 - core) * tile_cols, tile_cols, 0), "col", 0, "swap")
    most = tile_cols // 2
    pieces = [mine[:most], swapped[:most], mine[most:], swapped[most:]]
    hops, got = [], []

    ends = [tile[:, 0], tile[:, tile_cols - 1]]
    near = pairwise(jnp.where(core == 0, ends[1], ends[0]), "col", 0, "own_near")
    far = pairwise(jnp.where(core == 0, ends[0], ends[1]), "col", 1, "own_far")
    before, after = sides(near, far)
    ends = [
        jnp.concatenate([before[y : y + 1], tile[y], after[y : y + 1]]) for y in (0, tile_rows - 1)
    ]
    band_near = pairwise(jnp.where(up == 0, ends[1], ends[0]), "row", 0, "own_band_near")
    band_far = pairwise(jnp.where(up == 0, ends[0], ends[1]), "row", 1, "own_band_far")
    band_near, band_far, *pieces = lax.optimization_barrier((band_near, band_far, *pieces))
    for i, piece in enumerate(pieces):
        with jax.named_scope(f"hop{i}"):
            hops.append(place.hop(piece, (0, 1, 1, 0)[i]))
    for i, hop in enumerate(hops):
        with jax.named_scope(f"land{i}"):
            got.append(place.land(hop, (0, 1, 1, 0)[i]))
    first, ring, other_ring = call(
        "first",
        lambda *refs: first_kernel(*refs, step=divisor(tile_rows, 16)),
        (shape(tile_rows, tile_cols), *(shape(3 * tile_cols),) * 2),
        (tile, near, far, band_near, band_far, w_first),
        [
            scratch(tile_rows + 2, tile_cols + 2 * PAD, channels),
            scratch(tile_rows + 2, tile_cols, 3 * channels),
        ],
        tile_rows * tile_cols,
    )
    ring = jnp.concatenate([ring, pairwise(other_ring, "col", 0, "ring_swap")])
    with jax.named_scope("ring"):
        got_ring = place.direct(ring)
    (turned,) = call(
        "turned",
        lambda *refs: turned_kernel(*refs, step=divisor(tile_cols, 32)),
        (shape(tile_cols, tile_rows),),
        (*pieces, *got, w_first),
        [
            scratch(tile_cols + 2, tile_rows + 2 * PAD, channels),
            scratch(tile_cols + 2, tile_rows, 3 * channels),
        ],
        tile_rows * tile_cols,
    )
    sym, to_near, to_far = call(
        "mean",
        mean_kernel,
        (shape(tile_rows, tile_cols), shape(tile_rows, STRIP), shape(tile_rows, STRIP)),
        (first, turned, ring, got_ring),
        [scratch(tile_cols, tile_rows, channels), scratch(6 * tile_cols, channels)],
    )

    near = pairwise(to_near, "col", 0, "sym_near")
    far = pairwise(to_far, "col", 1, "sym_far")
    rows2, rows3 = tile_rows - 4, tile_rows - 2 * EDGE
    (inner,) = call(
        "inner_second",
        lambda *refs: inner_second_kernel(*refs, step=divisor(rows2, 30)),
        (shape(rows2, tile_cols),),
        (sym, w_second),
        [scratch(tile_rows, tile_cols, 3 * channels)],
        2 * rows2 * tile_cols,
    )
    before, after = sides(near, far)

    def band(at):
        return jnp.concatenate([cut(part, at, HALO, 0) for part in (before, sym, after)], axis=1)

    last = tile_rows - HALO
    band_near = pairwise(band((1 - up) * last), "row", 0, "sym_band_near")
    band_far = pairwise(band(up * last), "row", 1, "sym_band_far")
    width = tile_cols + 2 * STRIP
    step = divisor(rows3, 13)
    features, tops, bottoms = call(
        "middle",
        lambda *refs: middle_kernel(*refs, steps=(divisor(rows2, 30), step)),
        (shape(tile_rows, tile_cols), shape(STRIP, width), shape(STRIP, width)),
        (sym, near, far, inner, w_second, w_third),
        [
            scratch(tile_rows, tile_cols + 2 * PAD, channels),
            scratch(tile_rows, 16, 3 * channels),
            scratch(rows2, width, channels),
            scratch(rows2, tile_cols, 3 * channels),
            scratch(rows3, tile_cols, channels),
            pltpu.SemaphoreType.DMA((rows3 // step,)),
        ],
        2 * rows2 * 16 + rows3 * tile_cols,
        out_specs=(anywhere, *whole(2)),
    )
    return call(
        "edges",
        edges_kernel,
        (shape(tile_rows, tile_cols),),
        (features, sym, near, far, band_near, band_far, tops, bottoms, w_second, w_third),
        [
            scratch(2, HALO + 4, tile_cols + 2 * PAD, channels),
            scratch(2, HALO + 4, width, 3 * channels),
            scratch(2, HALO + STRIP, width, channels),
            scratch(2, HALO + STRIP, tile_cols, 3 * channels),
            scratch(2, EDGE, tile_cols, channels),
            pltpu.SemaphoreType.DMA((2,)),
        ],
        2 * 2 * HALO * width + 2 * EDGE * tile_cols,
        in_specs=[anywhere] + whole(9),
        out_specs=(anywhere,),
        alias={0: 0},
    )[0]


def solution(mesh):
    return jax.shard_map(
        local,
        mesh=mesh,
        in_specs=(P("row", "col", None), P(), P(), P()),
        out_specs=P("row", "col", None),
        check_vma=False,
    )
```

```python
import math

import jax
import jax.numpy as jnp
import numpy as np
from jax import lax
from jax.experimental import pallas as pl
from jax.experimental.pallas import tpu as pltpu
from jax.sharding import PartitionSpec as P

AXES = ("row", "col")
BF16, F32 = jnp.bfloat16, jnp.float32
PAD = 16
STRIP = 8
HALO = 6
EDGE = 6


def routes(row_count, plan):
    low = math.isqrt(row_count)
    first, second = {}, {}
    for r in range(row_count):
        for z in range(row_count):
            a, b, c, d = r // low, r % low, z // low, z % low
            if r == z:
                continue
            straight, across = (b == d, a == c) if plan == 0 else (a == c, b == d)
            turn = c * low + b if plan == 0 else a * low + d
            via = (r if straight else z if across else turn, z)
            first[(r, z)] = via
            second.setdefault(via, []).append((z, r))
    if any(len(ends) > 1 for ends in second.values()) or len(set(first.values())) < len(first):
        return {}, {(r, z): (z, r) for r in range(row_count) for z in range(row_count) if r != z}
    return first, {via: ends[0] for via, ends in second.items()}


class Place:
    def __init__(self):
        self.rows, self.cols = lax.axis_size("row"), lax.axis_size("col")
        self.row, self.col = lax.axis_index("row"), lax.axis_index("col")
        self.core = self.col % 2
        self.up = self.row % 2
        self.diagonal = self.row == self.col // 2
        self.legs = [routes(self.rows, plan) for plan in range(2)]

    def chips(self, array, legs):
        pairs = [
            (s[0] * self.cols + s[1] * 2 + k, e[0] * self.cols + e[1] * 2 + k)
            for s, e in legs.items()
            for k in range(2)
        ]
        return lax.ppermute(array, AXES, pairs)

    def hop(self, piece, plan):
        first = self.legs[plan][0]
        return self.chips(piece, first) if first else piece

    def direct(self, piece):
        places = [(r, z) for r in range(self.rows) for z in range(self.rows) if r != z]
        return self.chips(piece, {(r, z): (z, r) for r, z in places})

    def land(self, hopped, plan):
        return self.chips(hopped, self.legs[plan][1])


def pairwise(array, axis, start, name):
    size = lax.axis_size(axis)
    pairs = [(i, i + 1) for i in range(start, size - 1, 2)]
    if not pairs:
        return jnp.zeros_like(array)
    with jax.named_scope(name):
        return lax.ppermute(array, axis, pairs + [(j, i) for i, j in pairs])


def widen(wide, padded, start, width, step):
    channels = padded.shape[2]
    for q in range(3):
        at = start + q * step
        wide[:, :, q * channels : (q + 1) * channels] = padded[:, at : at + width, :]


def products(wide, weight, row, rows, step, flip=False):
    width, channels = wide.shape[1], wide.shape[2] // 3
    taps = [
        wide[pl.ds(row + p * step, rows), :, q * channels : (q + 1) * channels].reshape(
            rows * width, channels
        )
        for p in range(3)
        for q in range(3)
    ]
    if flip:
        taps = [taps[q * 3 + p] for p in range(3) for q in range(3)]
    flat = weight[...].reshape(9 * channels, weight.shape[3])
    return jnp.maximum(jnp.dot(jnp.concatenate(taps, axis=1), flat, preferred_element_type=F32), 0.0)


def sides(near, far):
    core = lax.axis_index("col") % 2
    return jnp.where(core == 0, far, near), jnp.where(core == 0, near, far)


def put_tile(padded, tile, near, far):
    rows, cols, channels = tile.shape
    padded[1 : 1 + rows, PAD : PAD + cols, :] = tile[...]
    before, after = sides(near[...], far[...])
    padded[1 : 1 + rows, PAD - 1 : PAD, :] = before.reshape(rows, 1, channels)
    padded[1 : 1 + rows, PAD + cols : PAD + cols + 1, :] = after.reshape(rows, 1, channels)


def first_kernel(tile, near, far, band_near, band_far, weight, out, mine, other, padded, wide, *, step):
    core, up = lax.axis_index("col") % 2, lax.axis_index("row") % 2
    rows, cols, channels = tile.shape
    put_tile(padded, tile, near, far)
    ends = slice(PAD - 1, PAD + cols + 1)
    padded[0, ends, :] = jnp.where(up == 0, band_far[...], band_near[...])
    padded[rows + 1, ends, :] = jnp.where(up == 0, band_near[...], band_far[...])
    widen(wide, padded, PAD - 1, cols, 1)
    for at in range(0, rows, step):
        value = products(wide, weight, at, step, 1)
        out[at : at + step] = value.astype(BF16).reshape(step, cols, channels)
    outer = jnp.where(core == 0, out[:, 0, :], out[:, cols - 1, :])
    for half in range(2):
        top = half * cols

        def put(ring, top=top):
            ring[:cols] = out[top]
            ring[cols : 2 * cols] = out[top + cols - 1]
            ring[2 * cols :] = outer[top : top + cols]

        pl.when(core == half)(lambda put=put: put(mine))
        pl.when(core != half)(lambda put=put: put(other))


def turned_kernel(kept0, kept1, kept2, kept3, got0, got1, got2, got3, weight, out, padded, wide, *, step):
    core = lax.axis_index("col") % 2
    diagonal = lax.axis_index("row") == lax.axis_index("col") // 2
    size, length, channels = out.shape
    rows = kept0.shape[0]

    def put(pieces):
        for side in range(2):
            left = PAD + side * size

            def fill(first, second, left=left):
                padded[1 : 1 + rows, left : left + size, :] = first[...]
                padded[1 + rows : 1 + size, left : left + size, :] = second[...]

            pl.when(core == side)(lambda fill=fill: fill(pieces[0], pieces[2]))
            pl.when(core != side)(lambda fill=fill: fill(pieces[1], pieces[3]))

    pl.when(diagonal)(lambda: put((kept0, kept1, kept2, kept3)))
    pl.when(jnp.logical_not(diagonal))(lambda: put((got0, got1, got2, got3)))
    widen(wide, padded, PAD - 1, length, 1)
    for at in range(0, size, step):
        value = products(wide, weight, at, step, 1)
        out[at : at + step] = value.astype(BF16).reshape(step, length, channels)


def mean_kernel(first, turned, kept, got, out, to_near, to_far):
    row, col = lax.axis_index("row"), lax.axis_index("col")
    core = col % 2
    size, length, channels = turned.shape
    ring = jnp.where(row == col // 2, kept[...], got[...])

    def mean(own, other):
        return ((own.astype(F32) + other.astype(F32)) * 0.5).astype(BF16)

    for side in range(2):
        rows = slice(side * size, (side + 1) * size)
        out[rows] = mean(first[rows], jnp.swapaxes(turned[:, rows, :], 0, 1))
        parts = [ring[at : at + size] for at in range(0, 6 * size, size)]
        upper, lower, outer = [jnp.where(core == side, parts[i], parts[i + 3]) for i in range(3)]
        for x, part in ((0, upper), (size - 1, lower)):
            place = slice(x, x + 1)
            out[rows, place, :] = mean(first[rows, place, :], part.reshape(size, 1, channels))
        edge = 0 if side == 0 else length - 1
        out[edge] = mean(first[edge], outer)
    start, end = out[:, :STRIP, :], out[:, size - STRIP :, :]
    to_near[...] = jnp.where(core == 0, end, start)
    to_far[...] = jnp.where(core == 0, start, end)


def second_rows(wide, weight, at, rows, valid):
    a = products(wide, weight, at, rows, 2).astype(BF16).astype(F32)
    b = products(wide, weight, at, rows, 2, flip=True).astype(BF16).astype(F32)
    mean = ((a + b) * 0.5).reshape(rows, wide.shape[1], -1)
    return jnp.where(valid, mean, 0.0).astype(BF16)


def columns_inside(x, tile_cols):
    x = x + lax.axis_index("col") * tile_cols
    return (x >= 0) & (x < tile_cols * lax.axis_size("col"))


def inner_second_kernel(sym, weight, out, wide, *, step):
    cols, channels = sym.shape[1], sym.shape[2]
    wide[:, 2:, :channels] = sym[:, : cols - 2, :]
    wide[:, :, channels : 2 * channels] = sym[...]
    wide[:, : cols - 2, 2 * channels :] = sym[:, 2:, :]
    for at in range(0, out.shape[0], step):
        out[at : at + step] = second_rows(wide, weight, at, step, True)


def middle_kernel(
    sym, near, far, inner, w_second, w_third, features, tops, bottoms, padded, wide2, sym2, wide3, out, done,
    *, steps
):
    tile_rows, tile_cols, channels = sym.shape
    end = PAD + tile_cols
    padded[:, PAD:end, :] = sym[...]
    before, after = sides(near[...], far[...])
    padded[:, PAD - STRIP : PAD, :] = before
    padded[:, end : end + STRIP, :] = after
    half = wide2.shape[1] // 2
    for q in range(3):
        lanes = slice(q * channels, (q + 1) * channels)
        at = PAD - 6 + 2 * q
        wide2[:, :half, lanes] = padded[:, at : at + half, :]
        at += tile_cols
        wide2[:, half:, lanes] = padded[:, at : at + half, :]
    x = lax.broadcasted_iota(jnp.int32, (1, 2 * half, 1), 1)
    valid = columns_inside(jnp.where(x < half, x - 4, x - half + tile_cols - 4), tile_cols)
    rows2, rows3 = sym2.shape[0], out.shape[0]
    sym2[:, STRIP : STRIP + tile_cols, :] = inner[...]
    for at in range(0, rows2, steps[0]):
        value = second_rows(wide2, w_second, at, steps[0], valid)
        rows = slice(at, at + steps[0])
        sym2[rows, STRIP - 4 : STRIP - 4 + half, :] = value[:, :half, :]
        to = STRIP + tile_cols - 4
        sym2[rows, to : to + half, :] = value[:, half:, :]
    tops[...] = sym2[0:STRIP]
    bottoms[...] = sym2[rows2 - STRIP : rows2]
    widen(wide3, sym2, STRIP - 4, tile_cols, 4)
    copies = []
    for i, at in enumerate(range(0, rows3, steps[1])):
        value = products(wide3, w_third, at, steps[1], 4)
        rows = pl.ds(at, steps[1])
        out[rows] = value.astype(BF16).reshape(steps[1], tile_cols, channels)
        target = features.at[pl.ds(EDGE + at, steps[1])]
        copies.append(pltpu.make_async_copy(out.at[rows], target, done.at[i]))
        copies[-1].start()
    for copy in copies:
        copy.wait()


def edges_kernel(
    _, sym, near, far, band_near, band_far, tops, bottoms, w_second, w_third, features,
    padded, wide2, sym2, wide3, out, done,
):
    row = lax.axis_index("row")
    up = row % 2
    tile_rows, tile_cols, channels = sym.shape
    end = PAD + tile_cols
    width = wide2.shape[2]
    side = (width - tile_cols) // 2
    x = lax.broadcasted_iota(jnp.int32, (1, width, 1), 1) - side
    valid = columns_inside(x, tile_cols)
    rows = padded.shape[1] - HALO
    bands = (
        jnp.where(up == 0, band_far[...], band_near[...]),
        jnp.where(up == 0, band_near[...], band_far[...]),
    )
    targets = [features.at[pl.ds(0, EDGE)], features.at[pl.ds(tile_rows - EDGE, EDGE)]]
    copies = [pltpu.make_async_copy(out.at[i], targets[i], done.at[i]) for i in range(2)]
    y = lax.broadcasted_iota(jnp.int32, (HALO, 1, 1), 0)
    insides = [
        row * tile_rows - 4 + y >= 0,
        (row + 1) * tile_rows - 2 + y < tile_rows * lax.axis_size("row"),
    ]
    for i in range(2):
        own = slice(HALO, HALO + rows) if i == 0 else slice(0, rows)
        outside = slice(0, HALO) if i == 0 else slice(rows, rows + HALO)
        source = slice(0, rows) if i == 0 else slice(tile_rows - rows, tile_rows)
        padded[i, own, PAD:end, :] = sym[source]
        before, after = sides(near[source], far[source])
        padded[i, own, PAD - STRIP : PAD, :] = before
        padded[i, own, end : end + STRIP, :] = after
        padded[i, outside, PAD - STRIP : end + STRIP, :] = bands[i]
        widen(wide2.at[i], padded.at[i], PAD - side - 2, width, 2)
    values = [second_rows(wide2.at[i], w_second, 0, HALO, valid & insides[i]) for i in range(2)]
    sym2[0, 0:HALO], sym2[0, HALO:] = values[0], tops[...]
    sym2[1, 0:STRIP], sym2[1, STRIP:] = bottoms[...], values[1]
    for i in range(2):
        widen(wide3.at[i], sym2.at[i], side - 4, tile_cols, 4)
    for i in range(2):
        value = products(wide3.at[i], w_third, 0, EDGE, 4)
        out[i] = value.astype(BF16).reshape(EDGE, tile_cols, channels)
        copies[i].start()
    for copy in copies:
        copy.wait()


def whole(count):
    return [pl.BlockSpec(memory_space=pltpu.VMEM)] * count


def divisor(number, most):
    return max(d for d in range(1, most + 1) if number % d == 0)


def cut(array, at, size, dim):
    return lax.dynamic_slice_in_dim(array, at, size, dim)


def local(contacts, w_first, w_second, w_third):
    tile_rows, tile_cols, channels = contacts.shape
    place = Place()
    core, up = place.core, place.up
    anywhere = pl.BlockSpec(memory_space=pl.ANY)

    def shape(*dims):
        return jax.ShapeDtypeStruct((*dims, channels), BF16)

    def scratch(*dims):
        return pltpu.VMEM(dims, BF16)

    def call(name, kernel, outs, ins, scratches, pixels=0, in_specs=None, out_specs=None, alias=None):
        macs = pixels * 9 * channels * channels
        return pl.pallas_call(
            kernel,
            out_shape=outs,
            in_specs=in_specs or whole(len(ins)),
            out_specs=out_specs or tuple(whole(len(outs))),
            scratch_shapes=scratches,
            input_output_aliases=alias or {},
            compiler_params=pltpu.CompilerParams(vmem_limit_bytes=24 * 2**20),
            cost_estimate=pl.CostEstimate(
                flops=2 * macs, bytes_accessed=18 * channels * channels, transcendentals=0
            ),
            name=name,
        )(*ins)

    tile = contacts
    mine = cut(tile, core * tile_cols, tile_cols, 0)
    swapped = pairwise(cut(tile, (1 - core) * tile_cols, tile_cols, 0), "col", 0, "swap")
    most = tile_cols // 2
    pieces = [mine[:most], swapped[:most], mine[most:], swapped[most:]]
    hops, got = [], []

    ends = [tile[:, 0], tile[:, tile_cols - 1]]
    near = pairwise(jnp.where(core == 0, ends[1], ends[0]), "col", 0, "own_near")
    far = pairwise(jnp.where(core == 0, ends[0], ends[1]), "col", 1, "own_far")
    before, after = sides(near, far)
    ends = [
        jnp.concatenate([before[y : y + 1], tile[y], after[y : y + 1]]) for y in (0, tile_rows - 1)
    ]
    band_near = pairwise(jnp.where(up == 0, ends[1], ends[0]), "row", 0, "own_band_near")
    band_far = pairwise(jnp.where(up == 0, ends[0], ends[1]), "row", 1, "own_band_far")
    band_near, band_far, *pieces = lax.optimization_barrier((band_near, band_far, *pieces))
    for i, piece in enumerate(pieces):
        with jax.named_scope(f"hop{i}"):
            hops.append(place.hop(piece, (0, 1, 1, 0)[i]))
    for i, hop in enumerate(hops):
        with jax.named_scope(f"land{i}"):
            got.append(place.land(hop, (0, 1, 1, 0)[i]))
    first, ring, other_ring = call(
        "first",
        lambda *refs: first_kernel(*refs, step=divisor(tile_rows, 16)),
        (shape(tile_rows, tile_cols), *(shape(3 * tile_cols),) * 2),
        (tile, near, far, band_near, band_far, w_first),
        [
            scratch(tile_rows + 2, tile_cols + 2 * PAD, channels),
            scratch(tile_rows + 2, tile_cols, 3 * channels),
        ],
        tile_rows * tile_cols,
    )
    ring = jnp.concatenate([ring, pairwise(other_ring, "col", 0, "ring_swap")])
    with jax.named_scope("ring"):
        got_ring = place.direct(ring)
    (turned,) = call(
        "turned",
        lambda *refs: turned_kernel(*refs, step=divisor(tile_cols, 32)),
        (shape(tile_cols, tile_rows),),
        (*pieces, *got, w_first),
        [
            scratch(tile_cols + 2, tile_rows + 2 * PAD, channels),
            scratch(tile_cols + 2, tile_rows, 3 * channels),
        ],
        tile_rows * tile_cols,
    )
    sym, to_near, to_far = call(
        "mean",
        mean_kernel,
        (shape(tile_rows, tile_cols), shape(tile_rows, STRIP), shape(tile_rows, STRIP)),
        (first, turned, ring, got_ring),
        [],
    )

    near = pairwise(to_near, "col", 0, "sym_near")
    far = pairwise(to_far, "col", 1, "sym_far")
    rows2, rows3 = tile_rows - 4, tile_rows - 2 * EDGE
    (inner,) = call(
        "inner_second",
        lambda *refs: inner_second_kernel(*refs, step=divisor(rows2, 30)),
        (shape(rows2, tile_cols),),
        (sym, w_second),
        [scratch(tile_rows, tile_cols, 3 * channels)],
        2 * rows2 * tile_cols,
    )
    before, after = sides(near, far)

    def band(at):
        return jnp.concatenate([cut(part, at, HALO, 0) for part in (before, sym, after)], axis=1)

    last = tile_rows - HALO
    band_near = pairwise(band((1 - up) * last), "row", 0, "sym_band_near")
    band_far = pairwise(band(up * last), "row", 1, "sym_band_far")
    width = tile_cols + 2 * STRIP
    step = divisor(rows3, 13)
    features, tops, bottoms = call(
        "middle",
        lambda *refs: middle_kernel(*refs, steps=(divisor(rows2, 30), step)),
        (shape(tile_rows, tile_cols), shape(STRIP, width), shape(STRIP, width)),
        (sym, near, far, inner, w_second, w_third),
        [
            scratch(tile_rows, tile_cols + 2 * PAD, channels),
            scratch(tile_rows, 16, 3 * channels),
            scratch(rows2, width, channels),
            scratch(rows2, tile_cols, 3 * channels),
            scratch(rows3, tile_cols, channels),
            pltpu.SemaphoreType.DMA((rows3 // step,)),
        ],
        2 * rows2 * 16 + rows3 * tile_cols,
        out_specs=(anywhere, *whole(2)),
    )
    return call(
        "edges",
        edges_kernel,
        (shape(tile_rows, tile_cols),),
        (features, sym, near, far, band_near, band_far, tops, bottoms, w_second, w_third),
        [
            scratch(2, HALO + 4, tile_cols + 2 * PAD, channels),
            scratch(2, HALO + 4, width, 3 * channels),
            scratch(2, HALO + STRIP, width, channels),
            scratch(2, HALO + STRIP, tile_cols, 3 * channels),
            scratch(2, EDGE, tile_cols, channels),
            pltpu.SemaphoreType.DMA((2,)),
        ],
        2 * 2 * HALO * width + 2 * EDGE * tile_cols,
        in_specs=[anywhere] + whole(9),
        out_specs=(anywhere,),
        alias={0: 0},
    )[0]


def solution(mesh):
    return jax.shard_map(
        local,
        mesh=mesh,
        in_specs=(P("row", "col", None), P(), P(), P()),
        out_specs=P("row", "col", None),
        check_vma=False,
    )
```
